32 devices in a mesh: gx: 4 (over z), gy: 4 (over y, x), gz: 2 (over core).
Axes of the slice: x: 2, y: 2, z: 4, core: 2. Of those that a mesh axis runs over, the one named last changes fastest.
Arguments:
- displacement: float32 [3, 128, 128, 512], P(None, 'gx', 'gy', 'gz'), may hold values from -0.0018 to 0.0018
- applied_strain: float32 [6], replicated, may hold values from -0.0003 to 0.0003
- labels: int32 [128, 128, 512], P('gx', 'gy', 'gz'), may hold values from 0 to 3
- history: float32 [128, 128, 512], P('gx', 'gy', 'gz'), may hold values from 5e-05 to 0.0006
- modulus: float32 [4], replicated, may hold values from 5000 to 60000
- poisson: float32 [4], replicated, may hold values from 0.1 to 0.3
- threshold: float32 [4], replicated, may hold values from 4e-05 to 0.00016
- ductility: float32 [4], replicated, may hold values from 0.6 to 1
- brittleness: float32 [4], replicated, may hold values from 5000 to 20000
- weight: float32 [4], replicated, may hold values from 0.1 to 1
Outputs:
- damage: float32 [128, 128, 512], P('gx', 'gy', 'gz')
- mises: float32 [128, 128, 512], P('gx', 'gy', 'gz')
The draws below stay inside these ranges and needn't reach their ends.
All inputs are finite; a program needn't handle non-finite values.
Results may differ from the reference program's by a relative error of at most 0.0003.
Values sent between devices are 32-bit elements; how exact they have to be, the bound alone decides.
A program may use at most 64 MiB of HBM per device.

```python
import math
import jax
import jax.numpy as jnp

RADIUS = 8
PHASES = 4
NX = 128
NY = 128
NZ = 512


def touch_ends(entries, stream_key, low, top_value):
    index_at = [jax.random.randint(jax.random.fold_in(stream_key, axis), (), 0, length) for axis, length in enumerate(entries.shape)]
    longest = entries.shape.index(max(entries.shape))
    next_to = index_at[:longest] + [(index_at[longest] + 1) % entries.shape[longest]] + index_at[longest + 1:]
    return entries.at[tuple(index_at)].set(low).at[tuple(next_to)].set(top_value)


def block_levels(stream_key, extent, split, low, largest):
    def one(axis_at, parts):
        draws = jax.random.uniform(jax.random.fold_in(jax.random.fold_in(stream_key, 6), axis_at), (parts,), jnp.float32, low / len(split), largest / len(split))
        return jnp.repeat(jnp.exp(draws), extent[axis_at] // parts).reshape((-1,) + (1,) * (len(extent) - axis_at - 1))

    level = one(*split[0])
    for cut in split[1:]:
        level = level * one(*cut)
    return level


def centred(stream_key, dims, deviation, reach, cuts=(), held_as=jnp.bfloat16):
    values = deviation * jax.random.normal(stream_key, dims, jnp.float32)
    if cuts:
        values = values * block_levels(stream_key, dims, cuts, -0.22, 0.18)
    return jnp.clip(values, -reach, reach).astype(held_as)


def setup_inputs(seed: int = 0) -> dict:
    keys = jax.random.split(jax.random.key(seed), 11)
    return {
        "displacement": centred(keys[0], (3, NX, NY, NZ), 0.0003, 0.0018, ((1, 4), (2, 4), (3, 2)), jnp.float32),
        "applied_strain": centred(keys[1], (6,), 0.0001, 0.0003, (), jnp.float32),
        "labels": touch_ends(jax.random.randint(keys[2], (NX, NY, NZ), 0, PHASES), jax.random.fold_in(keys[2], 1), 0, PHASES - 1).astype(jnp.int32),
        "history": jnp.clip(jnp.exp(math.log(0.0006) - 2.4849067 * jax.random.uniform(keys[3], (NX, NY, NZ), jnp.float32) ** block_levels(keys[3], (NX, NY, NZ), ((0, 4), (1, 4), (2, 2)), -0.2, 0.2)), 4.999999873689376e-05, 0.0006),
        "modulus": jnp.clip(jnp.exp(jax.random.uniform(keys[4], (PHASES,), jnp.float32, math.log(5000.0), math.log(60000.0))), 5000.0, 60000.0),
        "poisson": jnp.clip(jax.random.uniform(keys[5], (PHASES,), jnp.float32, 0.1, 0.3), 0.1, 0.3),
        "threshold": jnp.clip(jnp.exp(jax.random.uniform(keys[6], (PHASES,), jnp.float32, math.log(3.9999998989515007e-05), math.log(0.00016))), 3.9999998989515007e-05, 0.00016),
        "ductility": jnp.clip(jax.random.uniform(keys[7], (PHASES,), jnp.float32, 0.6, 1.0), 0.6, 1.0),
        "brittleness": jnp.clip(jnp.exp(jax.random.uniform(keys[8], (PHASES,), jnp.float32, math.log(5000.0), math.log(20000.0))), 5000.0, 20000.0),
        "weight": jnp.clip(jnp.exp(jax.random.uniform(keys[9], (PHASES,), jnp.float32, math.log(0.1), math.log(1.0))), 0.1, 1.0),
    }


def pick_phase(labels, table):
    picked = jnp.zeros(labels.shape, table.dtype)
    for which_phase in range(table.shape[0]):
        picked = jnp.where(labels == which_phase, table[which_phase], picked)
    return picked

def difference(field, along, others):
    result = jnp.roll(field, -1, along) - field
    for other in others:
        result = result + jnp.roll(result, -1, other)
    return 0.25 * result

def invariants(grad_x, grad_y, grad_z, applied_strain):
    strain_xx = applied_strain[0] + grad_x[0]
    strain_yy = applied_strain[1] + grad_y[1]
    strain_zz = applied_strain[2] + grad_z[2]
    strain_yz = applied_strain[3] + 0.5 * (grad_y[2] + grad_z[1])
    strain_xz = applied_strain[4] + 0.5 * (grad_x[2] + grad_z[0])
    strain_xy = applied_strain[5] + 0.5 * (grad_x[1] + grad_y[0])
    trace_strain = strain_xx + strain_yy + strain_zz
    second_inv = ((strain_xx - strain_yy) ** 2 + (strain_yy - strain_zz) ** 2 + (strain_zz - strain_xx) ** 2) / 6.0
    second_inv = second_inv + strain_yz * strain_yz + strain_xz * strain_xz + strain_xy * strain_xy
    return (trace_strain, second_inv)

def equivalent(trace_strain, second_inv, ratio_nu):
    ratio = 10.0
    lateral = (ratio - 1.0) / (1.0 - 2.0 * ratio_nu)
    under = lateral * lateral * trace_strain * trace_strain + 12.0 * ratio * second_inv / (1.0 + ratio_nu) ** 2
    return (lateral * trace_strain + jnp.sqrt(under)) / (2.0 * ratio)

def smooth_periodic(field, axis):
    total = None
    for offset in range(-RADIUS, RADIUS + 1):
        coeff = math.exp(-2.0 * offset * offset / (RADIUS * RADIUS))
        term = coeff * jnp.roll(field, -offset, axis)
        total = term if total is None else total + term
    return total

def finish(averaged, history, second_inv, labels, ratio_nu, modulus, threshold, ductility, brittleness):
    kappa = jnp.maximum(history, averaged)
    start = pick_phase(labels, threshold)
    ductile = pick_phase(labels, ductility)
    brittle = pick_phase(labels, brittleness)
    grown = 1.0 - start * (1.0 - ductile) / jnp.maximum(kappa, start) - ductile * jnp.exp(-brittle * (kappa - start))
    damage = jnp.where(kappa > start, grown, 0.0)
    stiff = pick_phase(labels, modulus)
    mises = (1.0 - damage) * stiff / (1.0 + ratio_nu) * jnp.sqrt(3.0 * second_inv)
    return (damage, mises)

def reference(displacement, applied_strain, labels, history, modulus, poisson, threshold, ductility, brittleness, weight):
    grad_x = difference(displacement, 1, (2, 3))
    grad_y = difference(displacement, 2, (1, 3))
    grad_z = difference(displacement, 3, (1, 2))
    trace_strain, second_inv = invariants(grad_x, grad_y, grad_z, applied_strain)
    ratio_nu = pick_phase(labels, poisson)
    equiv_strain = equivalent(trace_strain, second_inv, ratio_nu)
    weights_field = pick_phase(labels, weight)
    upper = weights_field * equiv_strain
    lower = weights_field
    for axis in range(3):
        upper = smooth_periodic(upper, axis)
        lower = smooth_periodic(lower, axis)
    averaged = upper / lower
    return finish(averaged, history, second_inv, labels, ratio_nu, modulus, threshold, ductility, brittleness)
```

```python
import functools
import math

import jax
import jax.numpy as jnp
from jax import lax
from jax.experimental import pallas as pl
from jax.experimental.pallas import tpu as pltpu
from jax.sharding import PartitionSpec as P

RADIUS = 8
LANES = 128
ROWS = 8
MESH = pl.DeviceIdType.MESH
TAPS = [math.exp(-2.0 * s * s / (RADIUS * RADIUS)) for s in range(RADIUS + 1)]
T_WEIGHT, T_LATERAL, T_FACTOR, T_WEIGHT_EQ, T_START, T_LOSS, T_DUCTILE, T_BRITTLE, T_STIFF = range(9)


def phase_masks(labels):
    return (labels == 0, labels == 1, labels == 2)


def pick(masks, tab, which):
    rows = [tab[pl.ds(4 * which + p, 1), : masks[0].shape[-1]] for p in range(4)]
    return jnp.where(
        masks[0], rows[0], jnp.where(masks[1], rows[1], jnp.where(masks[2], rows[2], rows[3]))
    )


def fill_tables(tab, modulus, poisson, threshold, ductility, brittleness, weight):
    width = tab.shape[-1]

    def put(which, phase, value):
        tab[4 * which + phase : 4 * which + phase + 1, :] = value

    for p in range(4):
        wide = lambda ref: jnp.full((1, width), ref[p], jnp.float32)
        nu, start, ductile, w = wide(poisson), wide(threshold), wide(ductility), wide(weight)
        put(T_WEIGHT, p, w)
        put(T_LATERAL, p, 9.0 / (1.0 - 2.0 * nu))
        put(T_FACTOR, p, 120.0 / ((1.0 + nu) * (1.0 + nu)))
        put(T_WEIGHT_EQ, p, w * 0.05)
        put(T_START, p, start)
        put(T_LOSS, p, start * (1.0 - ductile))
        put(T_DUCTILE, p, ductile)
        put(T_BRITTLE, p, -wide(brittleness))
        put(T_STIFF, p, wide(modulus) / (1.0 + nu) * math.sqrt(3.0))


def fill_bands(band_hi, band_lo):
    depth, width = band_hi.shape

    @pl.loop(0, depth // LANES)
    def _(i):
        rows = pl.ds(pl.multiple_of(i * LANES, LANES), LANES)
        k = lax.broadcasted_iota(jnp.int32, (LANES, width), 0) + i * LANES
        n = lax.broadcasted_iota(jnp.int32, (LANES, width), 1)
        d = (k - LANES - n).astype(jnp.float32)
        g = jnp.where(jnp.abs(d) <= RADIUS, jnp.exp(d * d * (-2.0 / (RADIUS * RADIUS))), 0.0)
        hi = g.astype(jnp.bfloat16)
        band_hi[rows, :] = hi
        band_lo[rows, :] = (g - hi.astype(jnp.float32)).astype(jnp.bfloat16)


def smooth_x(src, first, count):
    col = [src(first + i) for i in range(count + 2 * RADIUS)]
    outs = []
    for i in range(count):
        total = TAPS[0] * col[i + RADIUS]
        for s in range(1, RADIUS + 1):
            total = total + TAPS[s] * (col[i + RADIUS - s] + col[i + RADIUS + s])
        outs.append(total)
    return outs


def smooth_x_into(src, put, cells_x, cells_y):
    @pl.loop(0, cells_x // 8)
    def _(i):
        @pl.loop(0, cells_y // ROWS)
        def _(j):
            rows = pl.ds(pl.multiple_of(j * ROWS, ROWS), ROWS)
            outs = smooth_x(lambda x: src[i * 8 + x, rows, :], 0, 8)
            for x, value in enumerate(outs):
                put(i * 8 + x, rows, value)


def smooth_y(block):
    long = block.shape[0] - ROWS
    cells_y = block.shape[0] - 2 * RADIUS
    total = None
    for r in range(ROWS):
        part = None
        for q in range(3):
            s = ROWS * q + r
            if s > 2 * RADIUS:
                continue
            rows = cells_y if r == 0 else long
            term = TAPS[abs(s - RADIUS)] * block[ROWS * q : ROWS * q + rows]
            part = term if part is None else part + term
        if r:
            part = pltpu.roll(part, long - r, 0)[:cells_y]
        total = part if total is None else total + part
    return total


def smooth_z(planes, left, own, right, band_hi, band_lo):
    depth = band_hi.shape[0]
    cells_y = own.shape[1]
    rows = planes.size * cells_y
    block = jnp.concatenate([left[planes], own[planes], right[planes]], axis=2)
    block = block.reshape(rows, depth)
    hi = block.astype(jnp.bfloat16)
    lo = (block - hi.astype(jnp.float32)).astype(jnp.bfloat16)
    dot = functools.partial(jnp.dot, preferred_element_type=jnp.float32)
    out = dot(lo, band_hi[...]) + dot(hi, band_lo[...]) + dot(hi, band_hi[...])
    return out.reshape(planes.size, cells_y, out.shape[-1])


def kernel(
    disp, labels, history, strain0, modulus, poisson, threshold, ductility, brittleness, weight,
    damage_out, mises_out,
    ext, ysend, ybuf, ebuf, lab, hist, second, traw, tab, band_hi, band_lo,
    w_ax, w_ay, w_by, w_bx, t_ax, t_ay, t_by, t_bx,
    wfull, wl, wr, tl, tr, damage_v, mises_v,
    in_sem, out_sem, send_sem, recv_sem,
):
    cells_x, cells_y, cells_z = labels.shape
    half = cells_z // 2
    names = ("gx", "gy", "gz")
    count = {a: lax.axis_size(a) for a in names}
    here = {a: lax.axis_index(a) for a in names}

    def at(**moved):
        return tuple(lax.rem(here[a] + moved.get(a, 0) + count[a], count[a]) for a in names)

    x_up, x_down, y_up, y_down = at(gx=1), at(gx=-1), at(gy=1), at(gy=-1)
    z_up, z_down, d_up, d_down = at(gz=1), at(gz=-1), at(gx=1, gy=1), at(gx=-1, gy=-1)

    load_lab = pltpu.make_async_copy(labels, lab, in_sem.at[0])
    load_disp = pltpu.make_async_copy(
        disp, ext.at[:, pl.ds(0, cells_x), pl.ds(0, cells_y), pl.ds(0, cells_z)], in_sem.at[1]
    )
    load_hist = pltpu.make_async_copy(history, hist, in_sem.at[2])
    load_lab.start()
    load_disp.start()
    load_hist.start()

    barrier = pltpu.get_barrier_semaphore()
    greeted = (x_up, x_down, y_up, y_down, z_up, z_down, d_up, d_down)
    for device in greeted:
        pl.semaphore_signal(barrier, inc=1, device_id=device, device_id_type=MESH)

    slots = iter(range(send_sem.shape[0]))

    def remote(src, dst, device):
        slot = next(slots)
        copy = pltpu.make_async_remote_copy(
            src_ref=src, dst_ref=dst, send_sem=send_sem.at[slot], recv_sem=recv_sem.at[slot],
            device_id=device, device_id_type=MESH,
        )
        copy.start()
        return copy

    def halo_x(buf):
        return (
            remote(buf.at[pl.ds(RADIUS, RADIUS)], buf.at[pl.ds(cells_x + RADIUS, RADIUS)], x_down),
            remote(buf.at[pl.ds(cells_x, RADIUS)], buf.at[pl.ds(0, RADIUS)], x_up),
        )

    def halo_y(buf):
        return (
            remote(
                buf.at[:, pl.ds(RADIUS, RADIUS)], buf.at[:, pl.ds(cells_y + RADIUS, RADIUS)], y_down
            ),
            remote(buf.at[:, pl.ds(cells_y, RADIUS)], buf.at[:, pl.ds(0, RADIUS)], y_up),
        )

    def halo_z(buf, left, right):
        return (
            remote(buf.at[:, :, pl.ds(0, LANES)], right, z_down),
            remote(buf.at[:, :, pl.ds(cells_z - LANES, LANES)], left, z_up),
        )

    fill_tables(tab, modulus, poisson, threshold, ductility, brittleness, weight)
    load_lab.wait()

    @pl.loop(0, cells_x)
    def _(x):
        w = pick(phase_masks(lab[x]), tab, T_WEIGHT)
        w_ax[x + RADIUS] = w[:, :half]
        w_by[x, RADIUS : RADIUS + cells_y, :] = w[:, half:]

    load_disp.wait()

    @pl.loop(0, cells_x)
    def _(x):
        for c in range(3):
            ysend[c, pl.ds(x, 1), :] = ext[c, x, 0:1, :cells_z]

    pl.semaphore_wait(barrier, len(greeted))

    zcols = pl.ds(cells_z, LANES)
    first = pl.ds(0, LANES)
    ys = pl.ds(0, cells_y)
    node_x = remote(disp.at[:, 0], ext.at[:, cells_x, ys, pl.ds(0, cells_z)], x_down)
    node_y = remote(ysend, ybuf.at[:, :, pl.ds(0, cells_z)], y_down)
    node_e = remote(disp.at[:, 0, pl.ds(0, ROWS)], ebuf.at[:, :, pl.ds(0, cells_z)], d_down)
    node_z = remote(
        disp.at[:, :, :, first], ext.at[:, pl.ds(0, cells_x), ys, zcols], z_down
    )
    w1 = halo_x(w_ax) + halo_y(w_by)
    fill_bands(band_hi, band_lo)
    node_x.wait_recv()
    node_zx = remote(ext.at[:, cells_x, ys, first], ext.at[:, cells_x, ys, zcols], z_down)
    node_e.wait_recv()
    node_ze = remote(ebuf.at[:, :, first], ebuf.at[:, :, zcols], z_down)
    node_y.wait_recv()
    node_zy = remote(ybuf.at[:, :, first], ybuf.at[:, :, zcols], z_down)
    for copy in (node_z, node_zx, node_ze, node_zy):
        copy.wait_recv()

    wide = ext.shape[3]

    @pl.loop(0, cells_x)
    def _(x):
        for c in range(3):
            ext[c, x, cells_y : cells_y + ROWS, :] = jnp.broadcast_to(
                ybuf[c, pl.ds(x, 1), :], (ROWS, wide)
            )

    for c in range(3):
        ext[c, cells_x, cells_y : cells_y + ROWS, :] = jnp.broadcast_to(
            ebuf[c, 0:1, :], (ROWS, wide)
        )

    def strain_plane(x):
        gx, gy, gz = [], [], []
        rows = cells_y + ROWS

        def next_z(a):
            return pltpu.roll(a, wide - 1, 1)[:, :cells_z]

        def next_y(a):
            return pltpu.roll(a, rows - 1, 0)[:cells_y]

        for c in range(3):
            low, high = ext[c, x], ext[c, x + 1]
            diff, both = high - low, high + low
            diff = diff[:, :cells_z] + next_z(diff)
            moved = next_z(both)
            both = both[:, :cells_z]
            both, dz = both + moved, moved - both
            moved = next_y(both)
            gx.append(0.25 * (diff[:cells_y] + next_y(diff)))
            gy.append(0.25 * (moved - both[:cells_y]))
            gz.append(0.25 * (dz[:cells_y] + next_y(dz)))
        xx = strain0[0] + gx[0]
        yy = strain0[1] + gy[1]
        zz = strain0[2] + gz[2]
        yz = strain0[3] + 0.5 * (gy[2] + gz[1])
        xz = strain0[4] + 0.5 * (gx[2] + gz[0])
        xy = strain0[5] + 0.5 * (gx[1] + gy[0])
        trace = xx + yy + zz
        d1, d2, d3 = xx - yy, yy - zz, zz - xx
        inv = (d1 * d1 + d2 * d2 + d3 * d3) * (1.0 / 6.0) + yz * yz + xz * xz + xy * xy
        masks = phase_masks(lab[x])
        part = pick(masks, tab, T_LATERAL) * trace
        under = part * part + pick(masks, tab, T_FACTOR) * inv
        traw[x] = pick(masks, tab, T_WEIGHT_EQ) * (part + jnp.sqrt(under))
        second[x] = inv

    split = cells_x // 2
    pl.loop(0, split)(strain_plane)

    def put_ay(buf):
        def put(x, rows, value):
            buf[x, pl.ds(rows.start + RADIUS, ROWS), :] = value

        return put

    def first_smoothing(ax, ay, by, bx, copies):
        for copy in copies[:2]:
            copy.wait_recv()
        smooth_x_into(ax, put_ay(ay), cells_x, cells_y)
        sent = halo_y(ay)
        for copy in copies[2:]:
            copy.wait_recv()

        @pl.loop(0, cells_x)
        def _(x):
            bx[x + RADIUS] = smooth_y(by[x])

        return sent + halo_x(bx)

    def second_smoothing(ay, bx, full, copies):
        for copy in copies[:2]:
            copy.wait_recv()

        @pl.loop(0, cells_x)
        def _(x):
            full[x, :, :half] = smooth_y(ay[x])

        for copy in copies[2:]:
            copy.wait_recv()

        def put(x, rows, value):
            full[x, rows, half:] = value

        smooth_x_into(bx, put, cells_x, cells_y)

    w2 = first_smoothing(w_ax, w_ay, w_by, w_bx, w1)
    pl.loop(split, cells_x)(strain_plane)
    tz = halo_z(traw, tl, tr)
    for copy in tz:
        copy.wait_recv()
    step = 8

    @pl.loop(0, cells_x // step)
    def _(i):
        planes = pl.ds(i * step, step)
        out = smooth_z(planes, tl, traw, tr, band_hi, band_lo)
        t_ax[pl.ds(i * step + RADIUS, step)] = out[:, :, :half]
        t_by[planes, RADIUS : RADIUS + cells_y, :] = out[:, :, half:]

    t1 = halo_x(t_ax) + halo_y(t_by)
    second_smoothing(w_ay, w_bx, wfull, w2)
    wz = halo_z(wfull, wl, wr)
    t2 = first_smoothing(t_ax, t_ay, t_by, t_bx, t1)
    for copy in wz:
        copy.wait()
    for copy in tz:
        copy.wait_send()

    @pl.loop(0, cells_x // step)
    def _(i):
        planes = pl.ds(i * step, step)
        wfull[planes] = smooth_z(planes, wl, wfull, wr, band_hi, band_lo)

    load_hist.wait()
    second_smoothing(t_ay, t_bx, traw, t2)

    def finish_plane(x):
        masks = phase_masks(lab[x])
        kappa = jnp.maximum(hist[x], traw[x] / wfull[x])
        start = pick(masks, tab, T_START)
        grown = (
            1.0
            - pick(masks, tab, T_LOSS) / jnp.maximum(kappa, start)
            - pick(masks, tab, T_DUCTILE) * jnp.exp(pick(masks, tab, T_BRITTLE) * (kappa - start))
        )
        damage = jnp.where(kappa > start, grown, 0.0)
        damage_v[x] = damage
        mises_v[x] = (1.0 - damage) * pick(masks, tab, T_STIFF) * jnp.sqrt(second[x])

    stores = []
    for i in range(0, cells_x, step):
        pl.loop(i, i + step)(finish_plane)
        planes = pl.ds(i, step)
        for k, (src, dst) in enumerate(((damage_v, damage_out), (mises_v, mises_out))):
            copy = pltpu.make_async_copy(
                src.at[planes], dst.at[planes], out_sem.at[2 * (i // step) + k]
            )
            copy.start()
            stores.append(copy)
    for copy in stores:
        copy.wait()
    for copy in (node_x, node_y, node_e, node_z, node_zx, node_ze, node_zy) + w1 + w2 + t1 + t2:
        copy.wait_send()


def shards(
    displacement, applied_strain, labels, history,
    modulus, poisson, threshold, ductility, brittleness, weight,
):
    cells_x, cells_y, cells_z = labels.shape
    half = cells_z // 2
    f32 = functools.partial(pltpu.VMEM, dtype=jnp.float32)
    bf16 = functools.partial(pltpu.VMEM, dtype=jnp.bfloat16)
    full = (cells_x, cells_y, cells_z)
    long_x = (cells_x + 2 * RADIUS, cells_y, half)
    long_y = (cells_x, cells_y + 2 * RADIUS, half)
    tile = (cells_x, cells_y, LANES)
    wide = cells_z + LANES
    copies = 27
    scratch = [
        f32((3, cells_x + 1, cells_y + ROWS, wide)),
        f32((3, cells_x, cells_z)),
        f32((3, cells_x, wide)),
        f32((3, ROWS, wide)),
        pltpu.VMEM(full, jnp.int32),
        f32(full), f32(full), f32(full),
        f32((40, cells_z)),
        bf16((cells_z + 2 * LANES, cells_z)), bf16((cells_z + 2 * LANES, cells_z)),
        f32(long_x), f32(long_y), f32(long_y), f32(long_x),
        f32(long_x), f32(long_y), f32(long_y), f32(long_x),
        f32(full), f32(tile), f32(tile), f32(tile), f32(tile), f32(full), f32(full),
        pltpu.SemaphoreType.DMA((3,)),
        pltpu.SemaphoreType.DMA((2 * (cells_x // 8),)),
        pltpu.SemaphoreType.DMA((copies,)),
        pltpu.SemaphoreType.DMA((copies,)),
    ]
    whole = pl.BlockSpec(memory_space=pl.ANY)
    scalars = pl.BlockSpec(memory_space=pltpu.SMEM)
    out = jax.ShapeDtypeStruct(full, jnp.float32)
    return pl.pallas_call(
        kernel,
        out_shape=(out, out),
        in_specs=[whole] * 3 + [scalars] * 7,
        out_specs=(whole, whole),
        scratch_shapes=scratch,
        compiler_params=pltpu.CompilerParams(
            collective_id=0, has_side_effects=True, vmem_limit_bytes=56 * 1024 * 1024
        ),
        name="nonlocal_damage",
    )(
        displacement, labels, history, applied_strain,
        modulus, poisson, threshold, ductility, brittleness, weight,
    )


def solution(mesh):
    block = P("gx", "gy", "gz")
    placed = (P(None, "gx", "gy", "gz"), P(), block, block, P(), P(), P(), P(), P(), P())
    return jax.shard_map(
        shards, mesh=mesh, in_specs=placed, out_specs=(block, block), check_vma=False
    )
```

```python
import functools
import math

import jax
import jax.numpy as jnp
from jax import lax
from jax.experimental import pallas as pl
from jax.experimental.pallas import tpu as pltpu
from jax.sharding import PartitionSpec as P

RADIUS = 8
LANES = 128
ROWS = 8
MESH = pl.DeviceIdType.MESH
TAPS = [math.exp(-2.0 * s * s / (RADIUS * RADIUS)) for s in range(RADIUS + 1)]
T_WEIGHT, T_LATERAL, T_FACTOR, T_WEIGHT_EQ, T_STIFF = range(5)


def phase_masks(labels):
    return (labels == 0, labels == 1, labels == 2)


def pick(masks, tab, which):
    rows = [tab[pl.ds(4 * which + p, 1), : masks[0].shape[-1]] for p in range(4)]
    return jnp.where(
        masks[0], rows[0], jnp.where(masks[1], rows[1], jnp.where(masks[2], rows[2], rows[3]))
    )


def fill_tables(tab, modulus, poisson, weight):
    width = tab.shape[-1]

    def put(which, phase, value):
        tab[4 * which + phase : 4 * which + phase + 1, :] = value

    for p in range(4):
        wide = lambda ref: jnp.full((1, width), ref[p], jnp.float32)
        nu, w = wide(poisson), wide(weight)
        put(T_WEIGHT, p, w)
        put(T_LATERAL, p, 9.0 / (1.0 - 2.0 * nu))
        put(T_FACTOR, p, 120.0 / ((1.0 + nu) * (1.0 + nu)))
        put(T_WEIGHT_EQ, p, w * 0.05)
        put(T_STIFF, p, wide(modulus) / (1.0 + nu) * math.sqrt(3.0))


def fill_bands(band_hi, band_lo):
    depth, width = band_hi.shape

    @pl.loop(0, depth // LANES)
    def _(i):
        rows = pl.ds(pl.multiple_of(i * LANES, LANES), LANES)
        k = lax.broadcasted_iota(jnp.int32, (LANES, width), 0) + i * LANES
        n = lax.broadcasted_iota(jnp.int32, (LANES, width), 1)
        d = (k - LANES - n).astype(jnp.float32)
        g = jnp.where(jnp.abs(d) <= RADIUS, jnp.exp(d * d * (-2.0 / (RADIUS * RADIUS))), 0.0)
        hi = g.astype(jnp.bfloat16)
        band_hi[rows, :] = hi
        band_lo[rows, :] = (g - hi.astype(jnp.float32)).astype(jnp.bfloat16)


def smooth_x_own(src, dst, lanes):
    cells_x, cells_y, _ = src.shape

    @pl.loop(0, cells_y // ROWS)
    def _(j):
        rows = pl.ds(pl.multiple_of(j * ROWS, ROWS), ROWS)
        for first in range(0, cells_x, RADIUS):
            low, high = max(first - RADIUS, 0), min(first + 2 * RADIUS, cells_x)
            col = {x: src[x, rows, lanes] for x in range(low, high)}
            for x in range(first, first + RADIUS):
                total = TAPS[0] * col[x]
                for s in range(1, RADIUS + 1):
                    pair = [col[k] for k in (x - s, x + s) if k in col]
                    if pair:
                        total = total + TAPS[s] * (pair[0] + pair[1] if len(pair) > 1 else pair[0])
                dst[x, rows, lanes] = total


def smooth_x_halo(dst, low, high, lanes):
    cells_x, cells_y, _ = dst.shape

    @pl.loop(0, cells_y // ROWS)
    def _(j):
        rows = pl.ds(pl.multiple_of(j * ROWS, ROWS), ROWS)
        below = [low[k, rows, :] for k in range(RADIUS)]
        above = [high[k, rows, :] for k in range(RADIUS)]
        for i in range(RADIUS):
            total = dst[i, rows, lanes]
            for k in range(i, RADIUS):
                total = total + TAPS[i + RADIUS - k] * below[k]
            dst[i, rows, lanes] = total
            x = cells_x - RADIUS + i
            total = dst[x, rows, lanes]
            for k in range(i + 1):
                total = total + TAPS[RADIUS + k - i] * above[k]
            dst[x, rows, lanes] = total


def smooth_rows(block):
    long = block.shape[0] - ROWS
    cells_y = block.shape[0] - 2 * RADIUS
    total = None
    for r in range(ROWS):
        part = None
        for q in range(3):
            s = ROWS * q + r
            if s > 2 * RADIUS:
                continue
            rows = cells_y if r == 0 else long
            term = TAPS[abs(s - RADIUS)] * block[ROWS * q : ROWS * q + rows]
            part = term if part is None else part + term
        if r:
            part = pltpu.roll(part, long - r, 0)[:cells_y]
        total = part if total is None else total + part
    return total


def smooth_y_own(src, dst, lanes):
    cells_x = src.shape[0]

    @pl.loop(0, cells_x // 2)
    def _(i):
        for k in range(2):
            own = src[2 * i + k, :, lanes]
            edge = jnp.zeros((RADIUS, own.shape[1]), own.dtype)
            dst[2 * i + k, :, lanes] = smooth_rows(jnp.concatenate([edge, own, edge], axis=0))


def smooth_y_halo(dst, low, high, lanes):
    cells_x, cells_y, _ = dst.shape
    group = 8
    row = lax.broadcasted_iota(jnp.int32, (1, RADIUS, low.shape[2]), 1)

    @pl.loop(0, cells_x // group)
    def _(i):
        planes = pl.ds(i * group, group)
        below, above = low[planes], high[planes]
        first = dst[planes, 0:RADIUS, lanes]
        last = dst[planes, cells_y - RADIUS : cells_y, lanes]
        for d in range(RADIUS):
            tap = TAPS[RADIUS - d]
            if d == 0:
                first, last = first + tap * below, last + tap * above
            else:
                first = first + jnp.where(row < RADIUS - d, tap, 0.0) * pltpu.roll(
                    below, RADIUS - d, 1
                )
                last = last + jnp.where(row >= d, tap, 0.0) * pltpu.roll(above, d, 1)
        dst[planes, 0:RADIUS, lanes] = first
        dst[planes, cells_y - RADIUS : cells_y, lanes] = last


def banded(block, band_hi, band_lo):
    planes, cells_y, depth = block.shape
    block = block.reshape(planes * cells_y, depth)
    hi = block.astype(jnp.bfloat16)
    lo = (block - hi.astype(jnp.float32)).astype(jnp.bfloat16)
    dot = functools.partial(jnp.dot, preferred_element_type=jnp.float32)
    out = dot(lo, band_hi) + dot(hi, band_lo) + dot(hi, band_hi)
    return out.reshape(planes, cells_y, out.shape[-1])


def smooth_z_own(src, dst, band_hi, band_lo, group=8):
    own = pl.ds(LANES, src.shape[2])

    @pl.loop(0, src.shape[0] // group)
    def _(i):
        planes = pl.ds(i * group, group)
        dst[planes] = banded(src[planes], band_hi[own, :], band_lo[own, :])


def smooth_z_halo(dst, left, right, band_hi, band_lo, group=8):
    cells_z = dst.shape[2]
    first, last = pl.ds(0, LANES), pl.ds(cells_z - LANES, LANES)
    end = pl.ds(cells_z + LANES, LANES)

    @pl.loop(0, dst.shape[0] // group)
    def _(i):
        planes = pl.ds(i * group, group)
        dst[planes, :, first] += banded(left[planes], band_hi[first, first], band_lo[first, first])
        dst[planes, :, last] += banded(right[planes], band_hi[end, last], band_lo[end, last])


def kernel(
    disp, labels, strain0, modulus, poisson, weight,
    averaged_out, stress_out,
    ext, ysend, ybuf, ebuf, lab, second, tab, band_hi, band_lo,
    w_raw, w_one, w_two, w_z, t_raw, t_z, t_one, t_two,
    w_hx, w_hy, t_hx, t_hy, wl, wr, tl, tr,
    in_sem, out_sem, send_sem, recv_sem,
):
    cells_x, cells_y, cells_z = labels.shape
    half = cells_z // 2
    names = ("gx", "gy", "gz")
    count = {a: lax.axis_size(a) for a in names}
    here = {a: lax.axis_index(a) for a in names}

    def at(**moved):
        return tuple(lax.rem(here[a] + moved.get(a, 0) + count[a], count[a]) for a in names)

    x_up, x_down, y_up, y_down = at(gx=1), at(gx=-1), at(gy=1), at(gy=-1)
    z_up, z_down, d_up, d_down = at(gz=1), at(gz=-1), at(gx=1, gy=1), at(gx=-1, gy=-1)

    barrier = pltpu.get_barrier_semaphore()
    greeted = (x_up, x_down, y_up, y_down, z_up, z_down, d_up, d_down)
    for device in greeted:
        pl.semaphore_signal(barrier, inc=1, device_id=device, device_id_type=MESH)

    load_lab = pltpu.make_async_copy(labels, lab, in_sem.at[0])
    load_disp = pltpu.make_async_copy(
        disp, ext.at[:, pl.ds(0, cells_x), pl.ds(0, cells_y), pl.ds(0, cells_z)], in_sem.at[1]
    )
    load_lab.start()
    load_disp.start()

    slots = iter(range(send_sem.shape[0]))

    def remote(src, dst, device):
        slot = next(slots)
        copy = pltpu.make_async_remote_copy(
            src_ref=src, dst_ref=dst, send_sem=send_sem.at[slot], recv_sem=recv_sem.at[slot],
            device_id=device, device_id_type=MESH,
        )
        copy.start()
        return copy

    lower, upper = pl.ds(0, half), pl.ds(half, half)
    low, high = 0, 1

    def halo_x(buf, lanes, h, phase):
        return (
            remote(buf.at[pl.ds(0, RADIUS), :, lanes], h.at[phase, high], x_down),
            remote(buf.at[pl.ds(cells_x - RADIUS, RADIUS), :, lanes], h.at[phase, low], x_up),
        )

    def halo_y(buf, lanes, h, phase):
        return (
            remote(buf.at[:, pl.ds(0, RADIUS), lanes], h.at[phase, high], y_down),
            remote(buf.at[:, pl.ds(cells_y - RADIUS, RADIUS), lanes], h.at[phase, low], y_up),
        )

    def halo_z(buf, left, right, first, size):
        planes = pl.ds(first, size)
        return (
            remote(buf.at[planes, :, pl.ds(0, LANES)], right.at[planes], z_down),
            remote(buf.at[planes, :, pl.ds(cells_z - LANES, LANES)], left.at[planes], z_up),
        )

    fill_tables(tab, modulus, poisson, weight)
    pl.semaphore_wait(barrier, len(greeted))

    zcols = pl.ds(cells_z, LANES)
    first = pl.ds(0, LANES)
    ys = pl.ds(0, cells_y)
    node_x = remote(disp.at[:, 0], ext.at[:, cells_x, ys, pl.ds(0, cells_z)], x_down)
    node_e = remote(disp.at[:, 0, pl.ds(0, ROWS)], ebuf.at[:, :, pl.ds(0, cells_z)], d_down)
    node_z = remote(
        disp.at[:, :, :, first], ext.at[:, pl.ds(0, cells_x), ys, zcols], z_down
    )
    load_disp.wait()

    @pl.loop(0, cells_x)
    def _(x):
        for c in range(3):
            ysend[c, pl.ds(x, 1), :] = ext[c, x, 0:1, :cells_z]

    node_y = remote(ysend, ybuf.at[:, :, pl.ds(0, cells_z)], y_down)
    load_lab.wait()

    @pl.loop(0, cells_x)
    def _(x):
        w_raw[x] = pick(phase_masks(lab[x]), tab, T_WEIGHT)

    w1 = halo_x(w_raw, lower, w_hx, 0) + halo_y(w_raw, upper, w_hy, 0)
    fill_bands(band_hi, band_lo)
    node_x.wait_recv()
    node_zx = remote(ext.at[:, cells_x, ys, first], ext.at[:, cells_x, ys, zcols], z_down)
    node_e.wait_recv()
    node_ze = remote(ebuf.at[:, :, first], ebuf.at[:, :, zcols], z_down)
    node_y.wait_recv()
    node_zy = remote(ybuf.at[:, :, first], ybuf.at[:, :, zcols], z_down)
    smooth_x_own(w_raw, w_one, lower)
    smooth_y_own(w_raw, w_one, upper)
    for copy in (node_z, node_zx, node_ze, node_zy):
        copy.wait_recv()

    wide = ext.shape[3]

    @pl.loop(0, cells_x)
    def _(x):
        for c in range(3):
            ext[c, x, cells_y : cells_y + ROWS, :] = jnp.broadcast_to(
                ybuf[c, pl.ds(x, 1), :], (ROWS, wide)
            )

    for c in range(3):
        ext[c, cells_x, cells_y : cells_y + ROWS, :] = jnp.broadcast_to(
            ebuf[c, 0:1, :], (ROWS, wide)
        )

    def strain_plane(x):
        gx, gy, gz = [], [], []
        rows = cells_y + ROWS

        def next_z(a):
            return pltpu.roll(a, wide - 1, 1)[:, :cells_z]

        def next_y(a):
            return pltpu.roll(a, rows - 1, 0)[:cells_y]

        for c in range(3):
            low, high = ext[c, x], ext[c, x + 1]
            diff, both = high - low, high + low
            diff = diff[:, :cells_z] + next_z(diff)
            moved = next_z(both)
            both = both[:, :cells_z]
            both, dz = both + moved, moved - both
            moved = next_y(both)
            gx.append(0.25 * (diff[:cells_y] + next_y(diff)))
            gy.append(0.25 * (moved - both[:cells_y]))
            gz.append(0.25 * (dz[:cells_y] + next_y(dz)))
        xx = strain0[0] + gx[0]
        yy = strain0[1] + gy[1]
        zz = strain0[2] + gz[2]
        yz = strain0[3] + 0.5 * (gy[2] + gz[1])
        xz = strain0[4] + 0.5 * (gx[2] + gz[0])
        xy = strain0[5] + 0.5 * (gx[1] + gy[0])
        trace = xx + yy + zz
        d1, d2, d3 = xx - yy, yy - zz, zz - xx
        inv = (d1 * d1 + d2 * d2 + d3 * d3) * (1.0 / 6.0) + yz * yz + xz * xz + xy * xy
        masks = phase_masks(lab[x])
        part = pick(masks, tab, T_LATERAL) * trace
        under = part * part + pick(masks, tab, T_FACTOR) * inv
        t_raw[x] = pick(masks, tab, T_WEIGHT_EQ) * (part + jnp.sqrt(under))
        second[x] = inv

    def wait_recv(copies):
        for copy in copies:
            copy.wait_recv()

    split = cells_x // 2
    pl.loop(0, split)(strain_plane)
    tz = halo_z(t_raw, tl, tr, 0, split)
    wait_recv(w1)
    smooth_x_halo(w_one, w_hx.at[0, low], w_hx.at[0, high], lower)
    w2 = halo_y(w_one, lower, w_hy, 1)
    smooth_y_halo(w_one, w_hy.at[0, low], w_hy.at[0, high], upper)
    w2 += halo_x(w_one, upper, w_hx, 1)
    pl.loop(split, cells_x)(strain_plane)
    tz += halo_z(t_raw, tl, tr, split, cells_x - split)
    smooth_z_own(t_raw, t_z, band_hi, band_lo)
    wait_recv(tz)
    smooth_z_halo(t_z, tl, tr, band_hi, band_lo)
    t1 = halo_x(t_z, lower, t_hx, 0) + halo_y(t_z, upper, t_hy, 0)
    smooth_y_own(w_one, w_two, lower)
    smooth_x_own(w_one, w_two, upper)
    wait_recv(w2)
    smooth_y_halo(w_two, w_hy.at[1, low], w_hy.at[1, high], lower)
    smooth_x_halo(w_two, w_hx.at[1, low], w_hx.at[1, high], upper)
    wz = halo_z(w_two, wl, wr, 0, cells_x)
    smooth_x_own(t_z, t_one, lower)
    smooth_y_own(t_z, t_one, upper)
    wait_recv(t1)
    smooth_x_halo(t_one, t_hx.at[0, low], t_hx.at[0, high], lower)
    t2 = halo_y(t_one, lower, t_hy, 1)
    smooth_y_halo(t_one, t_hy.at[0, low], t_hy.at[0, high], upper)
    t2 += halo_x(t_one, upper, t_hx, 1)

    @pl.loop(0, cells_x)
    def _(x):
        second[x] = pick(phase_masks(lab[x]), tab, T_STIFF) * jnp.sqrt(second[x])

    store_stress = pltpu.make_async_copy(second, stress_out, out_sem.at[0])
    store_stress.start()
    smooth_z_own(w_two, w_z, band_hi, band_lo)
    wait_recv(wz)
    smooth_z_halo(w_z, wl, wr, band_hi, band_lo)
    smooth_y_own(t_one, t_two, lower)
    smooth_x_own(t_one, t_two, upper)

    @pl.loop(0, cells_x)
    def _(x):
        w_z[x] = 1.0 / w_z[x]

    wait_recv(t2)
    smooth_y_halo(t_two, t_hy.at[1, low], t_hy.at[1, high], lower)
    smooth_x_halo(t_two, t_hx.at[1, low], t_hx.at[1, high], upper)

    @pl.loop(0, cells_x)
    def _(x):
        t_two[x] = t_two[x] * w_z[x]

    store = pltpu.make_async_copy(t_two, averaged_out, out_sem.at[1])
    store.start()
    nodes = (node_x, node_y, node_e, node_z, node_zx, node_ze, node_zy)
    for copy in nodes + w1 + w2 + t1 + t2 + tz + wz:
        copy.wait_send()
    store_stress.wait()
    store.wait()


def finish(
    averaged, stress, labels, history, threshold, ductility, brittleness, damage_out, mises_out
):
    masks = phase_masks(labels[...])

    def chosen(ref):
        return jnp.where(
            masks[0], ref[0], jnp.where(masks[1], ref[1], jnp.where(masks[2], ref[2], ref[3]))
        )

    kappa = jnp.maximum(history[...], averaged[...])
    start, ductile, brittle = chosen(threshold), chosen(ductility), chosen(brittleness)
    grown = (
        1.0
        - start * (1.0 - ductile) / jnp.maximum(kappa, start)
        - ductile * jnp.exp(brittle * (start - kappa))
    )
    damage = jnp.where(kappa > start, grown, 0.0)
    damage_out[...] = damage
    mises_out[...] = (1.0 - damage) * stress[...]


def shards(
    displacement, applied_strain, labels, history,
    modulus, poisson, threshold, ductility, brittleness, weight,
):
    cells_x, cells_y, cells_z = labels.shape
    half = cells_z // 2
    f32 = functools.partial(pltpu.VMEM, dtype=jnp.float32)
    bf16 = functools.partial(pltpu.VMEM, dtype=jnp.bfloat16)
    full = (cells_x, cells_y, cells_z)
    tile = (cells_x, cells_y, LANES)
    halo_x = f32((2, 2, RADIUS, cells_y, half))
    halo_y = f32((2, 2, cells_x, RADIUS, half))
    wide = cells_z + LANES
    copies = 29
    scratch = [
        f32((3, cells_x + 1, cells_y + ROWS, wide)),
        f32((3, cells_x, cells_z)),
        f32((3, cells_x, wide)),
        f32((3, ROWS, wide)),
        pltpu.VMEM(full, jnp.int32),
        f32(full),
        f32((24, cells_z)),
        bf16((cells_z + 2 * LANES, cells_z)), bf16((cells_z + 2 * LANES, cells_z)),
        f32(full), f32(full), f32(full), f32(full), f32(full), f32(full), f32(full), f32(full),
        halo_x, halo_y, halo_x, halo_y,
        f32(tile), f32(tile), f32(tile), f32(tile),
        pltpu.SemaphoreType.DMA((2,)),
        pltpu.SemaphoreType.DMA((2,)),
        pltpu.SemaphoreType.DMA((copies,)),
        pltpu.SemaphoreType.DMA((copies,)),
    ]
    whole = pl.BlockSpec(memory_space=pl.ANY)
    scalars = pl.BlockSpec(memory_space=pltpu.SMEM)
    out = jax.ShapeDtypeStruct(full, jnp.float32)
    averaged, stress = pl.pallas_call(
        kernel,
        out_shape=(out, out),
        in_specs=[whole] * 2 + [scalars] * 4,
        out_specs=(whole, whole),
        scratch_shapes=scratch,
        compiler_params=pltpu.CompilerParams(
            collective_id=0, has_side_effects=True, vmem_limit_bytes=40 * 1024 * 1024
        ),
        name="strain_and_average",
    )(displacement, labels, applied_strain, modulus, poisson, weight)
    step = 8
    block = pl.BlockSpec((step, cells_y, cells_z), lambda i: (i, 0, 0))
    return pl.pallas_call(
        finish,
        grid=(cells_x // step,),
        out_shape=(out, out),
        in_specs=[block] * 4 + [scalars] * 3,
        out_specs=(block, block),
        compiler_params=pltpu.CompilerParams(vmem_limit_bytes=8 * 1024 * 1024),
        name="damage_and_stress",
    )(averaged, stress, labels, history, threshold, ductility, brittleness)


def solution(mesh):
    block = P("gx", "gy", "gz")
    placed = (P(None, "gx", "gy", "gz"), P(), block, block, P(), P(), P(), P(), P(), P())
    return jax.shard_map(
        shards, mesh=mesh, in_specs=placed, out_specs=(block, block), check_vma=False
    )
```

```python
import functools
import math

import jax
import jax.numpy as jnp
from jax import lax
from jax.experimental import pallas as pl
from jax.experimental.pallas import tpu as pltpu
from jax.sharding import PartitionSpec as P

RADIUS = 8
LANES = 128
ROWS = 8
MESH = pl.DeviceIdType.MESH
TAPS = [math.exp(-2.0 * s * s / (RADIUS * RADIUS)) for s in range(RADIUS + 1)]
T_WEIGHT, T_LATERAL, T_FACTOR, T_WEIGHT_EQ, T_STIFF = range(5)


def phase_masks(labels):
    return (labels == 0, labels == 1, labels == 2)


def pick(masks, tab, which):
    rows = [tab[pl.ds(4 * which + p, 1), : masks[0].shape[-1]] for p in range(4)]
    return jnp.where(
        masks[0], rows[0], jnp.where(masks[1], rows[1], jnp.where(masks[2], rows[2], rows[3]))
    )


def fill_tables(tab, modulus, poisson, weight):
    width = tab.shape[-1]

    def put(which, phase, value):
        tab[4 * which + phase : 4 * which + phase + 1, :] = value

    for p in range(4):
        wide = lambda ref: jnp.full((1, width), ref[p], jnp.float32)
        nu, w = wide(poisson), wide(weight)
        put(T_WEIGHT, p, w)
        put(T_LATERAL, p, 9.0 / (1.0 - 2.0 * nu))
        put(T_FACTOR, p, 120.0 / ((1.0 + nu) * (1.0 + nu)))
        put(T_WEIGHT_EQ, p, w * 0.05)
        put(T_STIFF, p, wide(modulus) / (1.0 + nu) * math.sqrt(3.0))


def fill_bands(band_hi, band_lo):
    depth, width = band_hi.shape

    @pl.loop(0, depth // LANES)
    def _(i):
        rows = pl.ds(pl.multiple_of(i * LANES, LANES), LANES)
        k = lax.broadcasted_iota(jnp.int32, (LANES, width), 0) + i * LANES
        n = lax.broadcasted_iota(jnp.int32, (LANES, width), 1)
        d = (k - LANES - n).astype(jnp.float32)
        g = jnp.where(jnp.abs(d) <= RADIUS, jnp.exp(d * d * (-2.0 / (RADIUS * RADIUS))), 0.0)
        hi = g.astype(jnp.bfloat16)
        band_hi[rows, :] = hi
        band_lo[rows, :] = (g - hi.astype(jnp.float32)).astype(jnp.bfloat16)


def smooth_x_own(src, dst, lanes):
    cells_x, cells_y, _ = src.shape

    @pl.loop(0, cells_y // ROWS)
    def _(j):
        rows = pl.ds(pl.multiple_of(j * ROWS, ROWS), ROWS)
        for first in range(0, cells_x, RADIUS):
            low, high = max(first - RADIUS, 0), min(first + 2 * RADIUS, cells_x)
            col = {x: src[x, rows, lanes] for x in range(low, high)}
            for x in range(first, first + RADIUS):
                total = TAPS[0] * col[x]
                for s in range(1, RADIUS + 1):
                    pair = [col[k] for k in (x - s, x + s) if k in col]
                    if pair:
                        total = total + TAPS[s] * (pair[0] + pair[1] if len(pair) > 1 else pair[0])
                dst[x, rows, lanes] = total


def smooth_x_halo(dst, low, high, lanes):
    cells_x, cells_y, _ = dst.shape

    @pl.loop(0, cells_y // ROWS)
    def _(j):
        rows = pl.ds(pl.multiple_of(j * ROWS, ROWS), ROWS)
        below = [low[k, rows, :] for k in range(RADIUS)]
        above = [high[k, rows, :] for k in range(RADIUS)]
        for i in range(RADIUS):
            total = dst[i, rows, lanes]
            for k in range(i, RADIUS):
                total = total + TAPS[i + RADIUS - k] * below[k]
            dst[i, rows, lanes] = total
            x = cells_x - RADIUS + i
            total = dst[x, rows, lanes]
            for k in range(i + 1):
                total = total + TAPS[RADIUS + k - i] * above[k]
            dst[x, rows, lanes] = total


def smooth_rows(block):
    long = block.shape[0] - ROWS
    cells_y = block.shape[0] - 2 * RADIUS
    total = None
    for r in range(ROWS):
        part = None
        for q in range(3):
            s = ROWS * q + r
            if s > 2 * RADIUS:
                continue
            rows = cells_y if r == 0 else long
            term = TAPS[abs(s - RADIUS)] * block[ROWS * q : ROWS * q + rows]
            part = term if part is None else part + term
        if r:
            part = pltpu.roll(part, long - r, 0)[:cells_y]
        total = part if total is None else total + part
    return total


def smooth_y_own(src, dst, lanes):
    cells_x = src.shape[0]

    @pl.loop(0, cells_x // 2)
    def _(i):
        for k in range(2):
            own = src[2 * i + k, :, lanes]
            edge = jnp.zeros((RADIUS, own.shape[1]), own.dtype)
            dst[2 * i + k, :, lanes] = smooth_rows(jnp.concatenate([edge, own, edge], axis=0))


def smooth_y_halo(dst, low, high, lanes):
    cells_x, cells_y, _ = dst.shape
    group = 8
    row = lax.broadcasted_iota(jnp.int32, (1, RADIUS, low.shape[2]), 1)

    @pl.loop(0, cells_x // group)
    def _(i):
        planes = pl.ds(i * group, group)
        below, above = low[planes], high[planes]
        first = dst[planes, 0:RADIUS, lanes]
        last = dst[planes, cells_y - RADIUS : cells_y, lanes]
        for d in range(RADIUS):
            tap = TAPS[RADIUS - d]
            if d == 0:
                first, last = first + tap * below, last + tap * above
            else:
                first = first + jnp.where(row < RADIUS - d, tap, 0.0) * pltpu.roll(
                    below, RADIUS - d, 1
                )
                last = last + jnp.where(row >= d, tap, 0.0) * pltpu.roll(above, d, 1)
        dst[planes, 0:RADIUS, lanes] = first
        dst[planes, cells_y - RADIUS : cells_y, lanes] = last


def banded(block, band_hi, band_lo):
    planes, cells_y, depth = block.shape
    block = block.reshape(planes * cells_y, depth)
    hi = block.astype(jnp.bfloat16)
    lo = (block - hi.astype(jnp.float32)).astype(jnp.bfloat16)
    dot = functools.partial(jnp.dot, preferred_element_type=jnp.float32)
    out = dot(lo, band_hi) + dot(hi, band_lo) + dot(hi, band_hi)
    return out.reshape(planes, cells_y, out.shape[-1])


def smooth_z_own(src, dst, band_hi, band_lo, group=8):
    own = pl.ds(LANES, src.shape[2])

    @pl.loop(0, src.shape[0] // group)
    def _(i):
        planes = pl.ds(i * group, group)
        dst[planes] = banded(src[planes], band_hi[own, :], band_lo[own, :])


def smooth_z_halo(dst, left, right, band_hi, band_lo, group=8):
    cells_z = dst.shape[2]
    first, last = pl.ds(0, LANES), pl.ds(cells_z - LANES, LANES)
    end = pl.ds(cells_z + LANES, LANES)

    @pl.loop(0, dst.shape[0] // group)
    def _(i):
        planes = pl.ds(i * group, group)
        dst[planes, :, first] += banded(left[planes], band_hi[first, first], band_lo[first, first])
        dst[planes, :, last] += banded(right[planes], band_hi[end, last], band_lo[end, last])


def kernel(
    disp, labels, strain0_in, modulus_in, poisson_in, weight_in,
    averaged_out, stress_out,
    strain0, modulus, poisson, weight,
    ext, ysend, ybuf, ebuf, lab, second, tab, band_hi, band_lo,
    w_raw, w_one, w_two, w_z, t_raw, t_z, t_one, t_two,
    w_hx, w_hy, t_hx, t_hy, wl, wr, tl, tr,
    in_sem, out_sem, send_sem, recv_sem,
):
    cells_x, cells_y, cells_z = labels.shape
    half = cells_z // 2
    names = ("gx", "gy", "gz")
    count = {a: lax.axis_size(a) for a in names}
    here = {a: lax.axis_index(a) for a in names}

    def at(**moved):
        return tuple(lax.rem(here[a] + moved.get(a, 0) + count[a], count[a]) for a in names)

    x_up, x_down, y_up, y_down = at(gx=1), at(gx=-1), at(gy=1), at(gy=-1)
    z_up, z_down, d_up, d_down = at(gz=1), at(gz=-1), at(gx=1, gy=1), at(gx=-1, gy=-1)

    barrier = pltpu.get_barrier_semaphore()
    greeted = (x_up, x_down, y_up, y_down, z_up, z_down, d_up, d_down)
    for device in greeted:
        pl.semaphore_signal(barrier, inc=1, device_id=device, device_id_type=MESH)

    load_lab = pltpu.make_async_copy(labels, lab, in_sem.at[0])
    load_disp = pltpu.make_async_copy(
        disp, ext.at[:, pl.ds(0, cells_x), pl.ds(0, cells_y), pl.ds(0, cells_z)], in_sem.at[1]
    )
    scalars = ((weight_in, weight), (poisson_in, poisson), (modulus_in, modulus),
               (strain0_in, strain0))
    load_scalars = [
        pltpu.make_async_copy(src, dst, in_sem.at[2 + i]) for i, (src, dst) in enumerate(scalars)
    ]
    for copy in load_scalars:
        copy.start()
    load_lab.start()
    load_disp.start()

    slots = iter(range(send_sem.shape[0]))

    def remote(src, dst, device):
        slot = next(slots)
        copy = pltpu.make_async_remote_copy(
            src_ref=src, dst_ref=dst, send_sem=send_sem.at[slot], recv_sem=recv_sem.at[slot],
            device_id=device, device_id_type=MESH,
        )
        copy.start()
        return copy

    lower, upper = pl.ds(0, half), pl.ds(half, half)
    low, high = 0, 1

    def halo_x(buf, lanes, h, phase):
        return (
            remote(buf.at[pl.ds(0, RADIUS), :, lanes], h.at[phase, high], x_down),
            remote(buf.at[pl.ds(cells_x - RADIUS, RADIUS), :, lanes], h.at[phase, low], x_up),
        )

    def halo_y(buf, lanes, h, phase):
        return (
            remote(buf.at[:, pl.ds(0, RADIUS), lanes], h.at[phase, high], y_down),
            remote(buf.at[:, pl.ds(cells_y - RADIUS, RADIUS), lanes], h.at[phase, low], y_up),
        )

    def halo_z(buf, left, right, first, size):
        planes = pl.ds(first, size)
        return (
            remote(buf.at[planes, :, pl.ds(0, LANES)], right.at[planes], z_down),
            remote(buf.at[planes, :, pl.ds(cells_z - LANES, LANES)], left.at[planes], z_up),
        )

    for copy in load_scalars:
        copy.wait()
    fill_tables(tab, modulus, poisson, weight)
    load_lab.wait()

    @pl.loop(0, cells_x)
    def _(x):
        w_raw[x] = pick(phase_masks(lab[x]), tab, T_WEIGHT)

    load_disp.wait()

    @pl.loop(0, cells_x)
    def _(x):
        for c in range(3):
            ysend[c, pl.ds(x, 1), :] = ext[c, x, 0:1, :cells_z]

    pl.semaphore_wait(barrier, len(greeted))

    zcols = pl.ds(cells_z, LANES)
    first = pl.ds(0, LANES)
    ys = pl.ds(0, cells_y)
    node_x = remote(disp.at[:, 0], ext.at[:, cells_x, ys, pl.ds(0, cells_z)], x_down)
    node_y = remote(ysend, ybuf.at[:, :, pl.ds(0, cells_z)], y_down)
    node_e = remote(disp.at[:, 0, pl.ds(0, ROWS)], ebuf.at[:, :, pl.ds(0, cells_z)], d_down)
    node_z = remote(
        disp.at[:, :, :, first], ext.at[:, pl.ds(0, cells_x), ys, zcols], z_down
    )
    w1 = halo_x(w_raw, lower, w_hx, 0) + halo_y(w_raw, upper, w_hy, 0)
    fill_bands(band_hi, band_lo)
    node_x.wait_recv()
    node_zx = remote(ext.at[:, cells_x, ys, first], ext.at[:, cells_x, ys, zcols], z_down)
    node_e.wait_recv()
    node_ze = remote(ebuf.at[:, :, first], ebuf.at[:, :, zcols], z_down)
    node_y.wait_recv()
    node_zy = remote(ybuf.at[:, :, first], ybuf.at[:, :, zcols], z_down)
    smooth_x_own(w_raw, w_one, lower)
    smooth_y_own(w_raw, w_one, upper)
    for copy in (node_z, node_zx, node_ze, node_zy):
        copy.wait_recv()

    wide = ext.shape[3]

    @pl.loop(0, cells_x)
    def _(x):
        for c in range(3):
            ext[c, x, cells_y : cells_y + ROWS, :] = jnp.broadcast_to(
                ybuf[c, pl.ds(x, 1), :], (ROWS, wide)
            )

    for c in range(3):
        ext[c, cells_x, cells_y : cells_y + ROWS, :] = jnp.broadcast_to(
            ebuf[c, 0:1, :], (ROWS, wide)
        )

    def strain_plane(x):
        gx, gy, gz = [], [], []
        rows = cells_y + ROWS

        def next_z(a):
            return pltpu.roll(a, wide - 1, 1)[:, :cells_z]

        def next_y(a):
            return pltpu.roll(a, rows - 1, 0)[:cells_y]

        for c in range(3):
            low, high = ext[c, x], ext[c, x + 1]
            diff, both = high - low, high + low
            diff = diff[:, :cells_z] + next_z(diff)
            moved = next_z(both)
            both = both[:, :cells_z]
            both, dz = both + moved, moved - both
            moved = next_y(both)
            gx.append(0.25 * (diff[:cells_y] + next_y(diff)))
            gy.append(0.25 * (moved - both[:cells_y]))
            gz.append(0.25 * (dz[:cells_y] + next_y(dz)))
        xx = strain0[0] + gx[0]
        yy = strain0[1] + gy[1]
        zz = strain0[2] + gz[2]
        yz = strain0[3] + 0.5 * (gy[2] + gz[1])
        xz = strain0[4] + 0.5 * (gx[2] + gz[0])
        xy = strain0[5] + 0.5 * (gx[1] + gy[0])
        trace = xx + yy + zz
        d1, d2, d3 = xx - yy, yy - zz, zz - xx
        inv = (d1 * d1 + d2 * d2 + d3 * d3) * (1.0 / 6.0) + yz * yz + xz * xz + xy * xy
        masks = phase_masks(lab[x])
        part = pick(masks, tab, T_LATERAL) * trace
        under = part * part + pick(masks, tab, T_FACTOR) * inv
        t_raw[x] = pick(masks, tab, T_WEIGHT_EQ) * (part + jnp.sqrt(under))
        second[x] = inv

    def wait_recv(copies):
        for copy in copies:
            copy.wait_recv()

    split = cells_x // 2
    pl.loop(0, split)(strain_plane)
    tz = halo_z(t_raw, tl, tr, 0, split)
    wait_recv(w1[:2])
    smooth_x_halo(w_one, w_hx.at[0, low], w_hx.at[0, high], lower)
    w2 = halo_y(w_one, lower, w_hy, 1)
    wait_recv(w1[2:])
    smooth_y_halo(w_one, w_hy.at[0, low], w_hy.at[0, high], upper)
    w2 += halo_x(w_one, upper, w_hx, 1)
    pl.loop(split, cells_x)(strain_plane)
    tz += halo_z(t_raw, tl, tr, split, cells_x - split)
    smooth_z_own(t_raw, t_z, band_hi, band_lo)
    wait_recv(tz)
    smooth_z_halo(t_z, tl, tr, band_hi, band_lo)
    t1 = halo_x(t_z, lower, t_hx, 0) + halo_y(t_z, upper, t_hy, 0)
    smooth_y_own(w_one, w_two, lower)
    smooth_x_own(w_one, w_two, upper)
    wait_recv(w2)
    smooth_y_halo(w_two, w_hy.at[1, low], w_hy.at[1, high], lower)
    smooth_x_halo(w_two, w_hx.at[1, low], w_hx.at[1, high], upper)
    wz = halo_z(w_two, wl, wr, 0, cells_x)
    smooth_x_own(t_z, t_one, lower)
    smooth_y_own(t_z, t_one, upper)
    wait_recv(t1[:2])
    smooth_x_halo(t_one, t_hx.at[0, low], t_hx.at[0, high], lower)
    t2 = halo_y(t_one, lower, t_hy, 1)
    wait_recv(t1[2:])
    smooth_y_halo(t_one, t_hy.at[0, low], t_hy.at[0, high], upper)
    t2 += halo_x(t_one, upper, t_hx, 1)

    @pl.loop(0, cells_x)
    def _(x):
        second[x] = pick(phase_masks(lab[x]), tab, T_STIFF) * jnp.sqrt(second[x])

    store_stress = pltpu.make_async_copy(second, stress_out, out_sem.at[0])
    store_stress.start()
    smooth_z_own(w_two, w_z, band_hi, band_lo)
    wait_recv(wz)
    smooth_z_halo(w_z, wl, wr, band_hi, band_lo)
    smooth_y_own(t_one, t_two, lower)
    smooth_x_own(t_one, t_two, upper)

    @pl.loop(0, cells_x)
    def _(x):
        w_z[x] = 1.0 / w_z[x]

    wait_recv(t2)
    smooth_y_halo(t_two, t_hy.at[1, low], t_hy.at[1, high], lower)
    smooth_x_halo(t_two, t_hx.at[1, low], t_hx.at[1, high], upper)

    @pl.loop(0, cells_x)
    def _(x):
        t_two[x] = t_two[x] * w_z[x]

    store = pltpu.make_async_copy(t_two, averaged_out, out_sem.at[1])
    store.start()
    nodes = (node_x, node_y, node_e, node_z, node_zx, node_ze, node_zy)
    for copy in nodes + w1 + w2 + t1 + t2 + tz + wz:
        copy.wait_send()
    store_stress.wait()
    store.wait()


def finish(
    averaged, stress, labels, history, threshold, ductility, brittleness, damage_out, mises_out
):
    masks = phase_masks(labels[...])

    def chosen(ref):
        return jnp.where(
            masks[0], ref[0], jnp.where(masks[1], ref[1], jnp.where(masks[2], ref[2], ref[3]))
        )

    kappa = jnp.maximum(history[...], averaged[...])
    start, ductile, brittle = chosen(threshold), chosen(ductility), chosen(brittleness)
    grown = (
        1.0
        - start * (1.0 - ductile) / jnp.maximum(kappa, start)
        - ductile * jnp.exp(brittle * (start - kappa))
    )
    damage = jnp.where(kappa > start, grown, 0.0)
    damage_out[...] = damage
    mises_out[...] = (1.0 - damage) * stress[...]


def shards(
    displacement, applied_strain, labels, history,
    modulus, poisson, threshold, ductility, brittleness, weight,
):
    cells_x, cells_y, cells_z = labels.shape
    half = cells_z // 2
    f32 = functools.partial(pltpu.VMEM, dtype=jnp.float32)
    bf16 = functools.partial(pltpu.VMEM, dtype=jnp.bfloat16)
    full = (cells_x, cells_y, cells_z)
    tile = (cells_x, cells_y, LANES)
    halo_x = f32((2, 2, RADIUS, cells_y, half))
    halo_y = f32((2, 2, cells_x, RADIUS, half))
    wide = cells_z + LANES
    copies = 29
    smem = functools.partial(pltpu.SMEM, dtype=jnp.float32)
    scratch = [
        smem(applied_strain.shape), smem(modulus.shape), smem(poisson.shape), smem(weight.shape),
        f32((3, cells_x + 1, cells_y + ROWS, wide)),
        f32((3, cells_x, cells_z)),
        f32((3, cells_x, wide)),
        f32((3, ROWS, wide)),
        pltpu.VMEM(full, jnp.int32),
        f32(full),
        f32((24, cells_z)),
        bf16((cells_z + 2 * LANES, cells_z)), bf16((cells_z + 2 * LANES, cells_z)),
        f32(full), f32(full), f32(full), f32(full), f32(full), f32(full), f32(full), f32(full),
        halo_x, halo_y, halo_x, halo_y,
        f32(tile), f32(tile), f32(tile), f32(tile),
        pltpu.SemaphoreType.DMA((6,)),
        pltpu.SemaphoreType.DMA((2,)),
        pltpu.SemaphoreType.DMA((copies,)),
        pltpu.SemaphoreType.DMA((copies,)),
    ]
    whole = pl.BlockSpec(memory_space=pl.ANY)
    scalars = pl.BlockSpec(memory_space=pltpu.SMEM)
    out = jax.ShapeDtypeStruct(full, jnp.float32)
    averaged, stress = pl.pallas_call(
        kernel,
        out_shape=(out, out),
        in_specs=[pl.BlockSpec(memory_space=pltpu.HBM)] * 6,
        out_specs=(whole, whole),
        scratch_shapes=scratch,
        compiler_params=pltpu.CompilerParams(
            collective_id=0, has_side_effects=True, vmem_limit_bytes=56 * 1024 * 1024
        ),
        name="strain_and_average",
    )(displacement, labels, applied_strain, modulus, poisson, weight)
    step = 8
    block = pl.BlockSpec((step, cells_y, cells_z), lambda i: (i, 0, 0))
    return pl.pallas_call(
        finish,
        grid=(cells_x // step,),
        out_shape=(out, out),
        in_specs=[block] * 4 + [scalars] * 3,
        out_specs=(block, block),
        compiler_params=pltpu.CompilerParams(vmem_limit_bytes=56 * 1024 * 1024),
        name="damage_and_stress",
    )(averaged, stress, labels, history, threshold, ductility, brittleness)


def solution(mesh):
    block = P("gx", "gy", "gz")
    placed = (P(None, "gx", "gy", "gz"), P(), block, block, P(), P(), P(), P(), P(), P())
    return jax.shard_map(
        shards, mesh=mesh, in_specs=placed, out_specs=(block, block), check_vma=False
    )
```

```python
import functools
import math

import jax
import jax.numpy as jnp
from jax import lax
from jax.experimental import pallas as pl
from jax.experimental.pallas import tpu as pltpu
from jax.sharding import PartitionSpec as P

RADIUS = 8
LANES = 128
ROWS = 8
MESH = pl.DeviceIdType.MESH
TAPS = [math.exp(-2.0 * s * s / (RADIUS * RADIUS)) for s in range(RADIUS + 1)]
T_WEIGHT, T_LATERAL, T_FACTOR, T_WEIGHT_EQ, T_STIFF = range(5)


def phase_masks(labels):
    return (labels == 0, labels == 1, labels == 2)


def pick(masks, tab, which):
    rows = [tab[pl.ds(4 * which + p, 1), : masks[0].shape[-1]] for p in range(4)]
    return jnp.where(
        masks[0], rows[0], jnp.where(masks[1], rows[1], jnp.where(masks[2], rows[2], rows[3]))
    )


def fill_tables(tab, modulus, poisson, weight):
    width = tab.shape[-1]

    def put(which, phase, value):
        tab[4 * which + phase : 4 * which + phase + 1, :] = value

    for p in range(4):
        wide = lambda ref: jnp.full((1, width), ref[p], jnp.float32)
        nu, w = wide(poisson), wide(weight)
        put(T_WEIGHT, p, w)
        put(T_LATERAL, p, 9.0 / (1.0 - 2.0 * nu))
        put(T_FACTOR, p, 120.0 / ((1.0 + nu) * (1.0 + nu)))
        put(T_WEIGHT_EQ, p, w * 0.05)
        put(T_STIFF, p, wide(modulus) / (1.0 + nu) * math.sqrt(3.0))


def fill_bands(band_hi, band_lo):
    depth, width = band_hi.shape

    @pl.loop(0, depth // LANES)
    def _(i):
        rows = pl.ds(pl.multiple_of(i * LANES, LANES), LANES)
        k = lax.broadcasted_iota(jnp.int32, (LANES, width), 0) + i * LANES
        n = lax.broadcasted_iota(jnp.int32, (LANES, width), 1)
        d = (k - LANES - n).astype(jnp.float32)
        g = jnp.where(jnp.abs(d) <= RADIUS, jnp.exp(d * d * (-2.0 / (RADIUS * RADIUS))), 0.0)
        hi = g.astype(jnp.bfloat16)
        band_hi[rows, :] = hi
        band_lo[rows, :] = (g - hi.astype(jnp.float32)).astype(jnp.bfloat16)


def smooth_x_own(src, dst, lanes):
    cells_x, cells_y, _ = src.shape

    @pl.loop(0, cells_y // ROWS)
    def _(j):
        rows = pl.ds(pl.multiple_of(j * ROWS, ROWS), ROWS)
        for first in range(0, cells_x, RADIUS):
            low, high = max(first - RADIUS, 0), min(first + 2 * RADIUS, cells_x)
            col = {x: src[x, rows, lanes] for x in range(low, high)}
            for x in range(first, first + RADIUS):
                total = TAPS[0] * col[x]
                for s in range(1, RADIUS + 1):
                    pair = [col[k] for k in (x - s, x + s) if k in col]
                    if pair:
                        total = total + TAPS[s] * (pair[0] + pair[1] if len(pair) > 1 else pair[0])
                dst[x, rows, lanes] = total


def ends_and_middle(count):
    return ((0, 1), (count - 1, count)), ((1, count - 1),)


def smooth_x_halo(dst, low, high, lanes, spans):
    cells_x, cells_y, _ = dst.shape

    def step(j):
        rows = pl.ds(pl.multiple_of(j * ROWS, ROWS), ROWS)
        below = [low[k, rows, :] for k in range(RADIUS)]
        above = [high[k, rows, :] for k in range(RADIUS)]
        for i in range(RADIUS):
            total = dst[i, rows, lanes]
            for k in range(i, RADIUS):
                total = total + TAPS[i + RADIUS - k] * below[k]
            dst[i, rows, lanes] = total
            x = cells_x - RADIUS + i
            total = dst[x, rows, lanes]
            for k in range(i + 1):
                total = total + TAPS[RADIUS + k - i] * above[k]
            dst[x, rows, lanes] = total

    for span in spans:
        pl.loop(*span)(step)


def smooth_rows(block):
    long = block.shape[0] - ROWS
    cells_y = block.shape[0] - 2 * RADIUS
    total = None
    for r in range(ROWS):
        part = None
        for q in range(3):
            s = ROWS * q + r
            if s > 2 * RADIUS:
                continue
            rows = cells_y if r == 0 else long
            term = TAPS[abs(s - RADIUS)] * block[ROWS * q : ROWS * q + rows]
            part = term if part is None else part + term
        if r:
            part = pltpu.roll(part, long - r, 0)[:cells_y]
        total = part if total is None else total + part
    return total


def smooth_y_own(src, dst, lanes):
    cells_x = src.shape[0]

    @pl.loop(0, cells_x // 2)
    def _(i):
        for k in range(2):
            own = src[2 * i + k, :, lanes]
            edge = jnp.zeros((RADIUS, own.shape[1]), own.dtype)
            dst[2 * i + k, :, lanes] = smooth_rows(jnp.concatenate([edge, own, edge], axis=0))


def smooth_y_halo(dst, low, high, lanes, spans):
    cells_x, cells_y, _ = dst.shape
    group = 8
    row = lax.broadcasted_iota(jnp.int32, (1, RADIUS, low.shape[2]), 1)

    def step(i):
        planes = pl.ds(i * group, group)
        below, above = low[planes], high[planes]
        first = dst[planes, 0:RADIUS, lanes]
        last = dst[planes, cells_y - RADIUS : cells_y, lanes]
        for d in range(RADIUS):
            tap = TAPS[RADIUS - d]
            if d == 0:
                first, last = first + tap * below, last + tap * above
            else:
                first = first + jnp.where(row < RADIUS - d, tap, 0.0) * pltpu.roll(
                    below, RADIUS - d, 1
                )
                last = last + jnp.where(row >= d, tap, 0.0) * pltpu.roll(above, d, 1)
        dst[planes, 0:RADIUS, lanes] = first
        dst[planes, cells_y - RADIUS : cells_y, lanes] = last

    for span in spans:
        pl.loop(*span)(step)


def banded(block, band_hi, band_lo):
    planes, cells_y, depth = block.shape
    block = block.reshape(planes * cells_y, depth)
    hi = block.astype(jnp.bfloat16)
    lo = (block - hi.astype(jnp.float32)).astype(jnp.bfloat16)
    dot = functools.partial(jnp.dot, preferred_element_type=jnp.float32)
    out = dot(lo, band_hi) + dot(hi, band_lo) + dot(hi, band_hi)
    return out.reshape(planes, cells_y, out.shape[-1])


def smooth_z_own(src, dst, band_hi, band_lo, group=8):
    own = pl.ds(LANES, src.shape[2])

    @pl.loop(0, src.shape[0] // group)
    def _(i):
        planes = pl.ds(i * group, group)
        dst[planes] = banded(src[planes], band_hi[own, :], band_lo[own, :])


def smooth_z_halo(dst, left, right, band_hi, band_lo, group=8):
    cells_z = dst.shape[2]
    first, last = pl.ds(0, LANES), pl.ds(cells_z - LANES, LANES)
    end = pl.ds(cells_z + LANES, LANES)

    @pl.loop(0, dst.shape[0] // group)
    def _(i):
        planes = pl.ds(i * group, group)
        dst[planes, :, first] += banded(left[planes], band_hi[first, first], band_lo[first, first])
        dst[planes, :, last] += banded(right[planes], band_hi[end, last], band_lo[end, last])


def kernel(
    disp, labels, history, strain0_in, modulus_in, poisson_in, weight_in,
    kappa_out, stress_out,
    strain0, modulus, poisson, weight,
    ext, edge, ysend, ybuf, ebuf, lab, hist, second, tab, band_hi, band_lo,
    w_raw, w_one, w_two, w_z, t_raw, t_z, t_one, t_two,
    w_hx, w_hy, t_hx, t_hy, wl, wr, tl, tr,
    in_sem, out_sem, send_sem, recv_sem,
):
    cells_x, cells_y, cells_z = labels.shape
    half = cells_z // 2
    names = ("gx", "gy", "gz")
    count = {a: lax.axis_size(a) for a in names}
    here = {a: lax.axis_index(a) for a in names}

    def at(**moved):
        return tuple(lax.rem(here[a] + moved.get(a, 0) + count[a], count[a]) for a in names)

    x_up, x_down, y_up, y_down = at(gx=1), at(gx=-1), at(gy=1), at(gy=-1)
    z_up, z_down, d_up, d_down = at(gz=1), at(gz=-1), at(gx=1, gy=1), at(gx=-1, gy=-1)

    barrier = pltpu.get_barrier_semaphore()
    greeted = (x_up, x_down, y_up, y_down, z_up, z_down, d_up, d_down)
    for device in greeted:
        pl.semaphore_signal(barrier, inc=1, device_id=device, device_id_type=MESH)

    load_lab = pltpu.make_async_copy(labels, lab, in_sem.at[0])
    load_disp = pltpu.make_async_copy(
        disp, ext.at[:, pl.ds(0, cells_x), pl.ds(0, cells_y), pl.ds(0, cells_z)], in_sem.at[1]
    )
    scalars = ((weight_in, weight), (poisson_in, poisson), (modulus_in, modulus),
               (strain0_in, strain0))
    load_scalars = [
        pltpu.make_async_copy(src, dst, in_sem.at[2 + i]) for i, (src, dst) in enumerate(scalars)
    ]
    for copy in load_scalars:
        copy.start()
    load_edge = pltpu.make_async_copy(disp.at[:, :, pl.ds(0, ROWS)], edge, in_sem.at[6])
    load_hist = pltpu.make_async_copy(history, hist, in_sem.at[7])
    for copy in (load_edge, load_lab, load_disp, load_hist):
        copy.start()

    slots = iter(range(send_sem.shape[0]))

    def remote(src, dst, device):
        slot = next(slots)
        copy = pltpu.make_async_remote_copy(
            src_ref=src, dst_ref=dst, send_sem=send_sem.at[slot], recv_sem=recv_sem.at[slot],
            device_id=device, device_id_type=MESH,
        )
        copy.start()
        return copy

    lower, upper = pl.ds(0, half), pl.ds(half, half)
    low, high = 0, 1

    def halo_x(buf, lanes, h, phase):
        return (
            remote(buf.at[pl.ds(0, RADIUS), :, lanes], h.at[phase, high], x_down),
            remote(buf.at[pl.ds(cells_x - RADIUS, RADIUS), :, lanes], h.at[phase, low], x_up),
        )

    def halo_y(buf, lanes, h, phase):
        return (
            remote(buf.at[:, pl.ds(0, RADIUS), lanes], h.at[phase, high], y_down),
            remote(buf.at[:, pl.ds(cells_y - RADIUS, RADIUS), lanes], h.at[phase, low], y_up),
        )

    def halo_z(buf, left, right, first, size):
        planes = pl.ds(first, size)
        return (
            remote(buf.at[planes, :, pl.ds(0, LANES)], right.at[planes], z_down),
            remote(buf.at[planes, :, pl.ds(cells_z - LANES, LANES)], left.at[planes], z_up),
        )

    load_edge.wait()

    @pl.loop(0, cells_x)
    def _(x):
        for c in range(3):
            ysend[c, pl.ds(x, 1), :] = edge[c, x, 0:1, :]

    zcols = pl.ds(cells_z, LANES)
    first = pl.ds(0, LANES)
    ys = pl.ds(0, cells_y)
    pl.semaphore_wait(barrier, len(greeted))
    node_x = remote(disp.at[:, 0], ext.at[:, cells_x, ys, pl.ds(0, cells_z)], x_down)
    node_y = remote(ysend, ybuf.at[:, :, pl.ds(0, cells_z)], y_down)
    node_e = remote(disp.at[:, 0, pl.ds(0, ROWS)], ebuf.at[:, :, pl.ds(0, cells_z)], d_down)
    node_z = remote(
        disp.at[:, :, :, first], ext.at[:, pl.ds(0, cells_x), ys, zcols], z_down
    )
    for copy in load_scalars:
        copy.wait()
    fill_tables(tab, modulus, poisson, weight)
    load_lab.wait()

    @pl.loop(0, cells_x)
    def _(x):
        w_raw[x] = pick(phase_masks(lab[x]), tab, T_WEIGHT)

    w1 = halo_x(w_raw, lower, w_hx, 0) + halo_y(w_raw, upper, w_hy, 0)
    fill_bands(band_hi, band_lo)
    node_x.wait_recv()
    node_zx = remote(ext.at[:, cells_x, ys, first], ext.at[:, cells_x, ys, zcols], z_down)
    node_e.wait_recv()
    node_ze = remote(ebuf.at[:, :, first], ebuf.at[:, :, zcols], z_down)
    node_y.wait_recv()
    node_zy = remote(ybuf.at[:, :, first], ybuf.at[:, :, zcols], z_down)
    smooth_x_own(w_raw, w_one, lower)
    smooth_y_own(w_raw, w_one, upper)
    for copy in (node_z, node_zx, node_ze, node_zy):
        copy.wait_recv()

    wide = ext.shape[3]
    load_disp.wait()

    @pl.loop(0, cells_x)
    def _(x):
        for c in range(3):
            ext[c, x, cells_y : cells_y + ROWS, :] = jnp.broadcast_to(
                ybuf[c, pl.ds(x, 1), :], (ROWS, wide)
            )

    for c in range(3):
        ext[c, cells_x, cells_y : cells_y + ROWS, :] = jnp.broadcast_to(
            ebuf[c, 0:1, :], (ROWS, wide)
        )

    def strain_plane(x):
        gx, gy, gz = [], [], []
        rows = cells_y + ROWS

        def next_z(a):
            return pltpu.roll(a, wide - 1, 1)[:, :cells_z]

        def next_y(a):
            return pltpu.roll(a, rows - 1, 0)[:cells_y]

        for c in range(3):
            low, high = ext[c, x], ext[c, x + 1]
            diff, both = high - low, high + low
            diff = diff[:, :cells_z] + next_z(diff)
            moved = next_z(both)
            both = both[:, :cells_z]
            both, dz = both + moved, moved - both
            moved = next_y(both)
            gx.append(0.25 * (diff[:cells_y] + next_y(diff)))
            gy.append(0.25 * (moved - both[:cells_y]))
            gz.append(0.25 * (dz[:cells_y] + next_y(dz)))
        xx = strain0[0] + gx[0]
        yy = strain0[1] + gy[1]
        zz = strain0[2] + gz[2]
        yz = strain0[3] + 0.5 * (gy[2] + gz[1])
        xz = strain0[4] + 0.5 * (gx[2] + gz[0])
        xy = strain0[5] + 0.5 * (gx[1] + gy[0])
        trace = xx + yy + zz
        d1, d2, d3 = xx - yy, yy - zz, zz - xx
        inv = (d1 * d1 + d2 * d2 + d3 * d3) * (1.0 / 6.0) + yz * yz + xz * xz + xy * xy
        masks = phase_masks(lab[x])
        part = pick(masks, tab, T_LATERAL) * trace
        under = part * part + pick(masks, tab, T_FACTOR) * inv
        t_raw[x] = pick(masks, tab, T_WEIGHT_EQ) * (part + jnp.sqrt(under))
        second[x] = inv

    row_ends, row_middle = ends_and_middle(cells_y // ROWS)
    plane_ends, plane_middle = ends_and_middle(cells_x // 8)

    def wait_recv(copies):
        for copy in copies:
            copy.wait_recv()

    split = cells_x // 2
    pl.loop(0, split)(strain_plane)
    tz = halo_z(t_raw, tl, tr, 0, split)
    wait_recv(w1[:2])
    smooth_x_halo(w_one, w_hx.at[0, low], w_hx.at[0, high], lower, row_ends)
    w2 = halo_y(w_one, lower, w_hy, 1)
    wait_recv(w1[2:])
    smooth_y_halo(w_one, w_hy.at[0, low], w_hy.at[0, high], upper, plane_ends)
    w2 += halo_x(w_one, upper, w_hx, 1)
    smooth_x_halo(w_one, w_hx.at[0, low], w_hx.at[0, high], lower, row_middle)
    smooth_y_halo(w_one, w_hy.at[0, low], w_hy.at[0, high], upper, plane_middle)
    pl.loop(split, cells_x)(strain_plane)
    tz += halo_z(t_raw, tl, tr, split, cells_x - split)
    smooth_z_own(t_raw, t_z, band_hi, band_lo)
    wait_recv(tz)
    smooth_z_halo(t_z, tl, tr, band_hi, band_lo)
    t1 = halo_x(t_z, lower, t_hx, 0) + halo_y(t_z, upper, t_hy, 0)
    smooth_y_own(w_one, w_two, lower)
    smooth_x_own(w_one, w_two, upper)
    wait_recv(w2)
    smooth_y_halo(w_two, w_hy.at[1, low], w_hy.at[1, high], lower, plane_ends + plane_middle)
    smooth_x_halo(w_two, w_hx.at[1, low], w_hx.at[1, high], upper, row_ends + row_middle)
    wz = halo_z(w_two, wl, wr, 0, cells_x)
    smooth_x_own(t_z, t_one, lower)
    smooth_y_own(t_z, t_one, upper)
    wait_recv(t1[:2])
    smooth_x_halo(t_one, t_hx.at[0, low], t_hx.at[0, high], lower, row_ends)
    t2 = halo_y(t_one, lower, t_hy, 1)
    wait_recv(t1[2:])
    smooth_y_halo(t_one, t_hy.at[0, low], t_hy.at[0, high], upper, plane_ends)
    t2 += halo_x(t_one, upper, t_hx, 1)
    smooth_x_halo(t_one, t_hx.at[0, low], t_hx.at[0, high], lower, row_middle)
    smooth_y_halo(t_one, t_hy.at[0, low], t_hy.at[0, high], upper, plane_middle)

    @pl.loop(0, cells_x)
    def _(x):
        second[x] = pick(phase_masks(lab[x]), tab, T_STIFF) * jnp.sqrt(second[x])

    store_stress = pltpu.make_async_copy(second, stress_out, out_sem.at[0])
    store_stress.start()
    smooth_z_own(w_two, w_z, band_hi, band_lo)
    wait_recv(wz)
    smooth_z_halo(w_z, wl, wr, band_hi, band_lo)
    smooth_y_own(t_one, t_two, lower)
    smooth_x_own(t_one, t_two, upper)

    @pl.loop(0, cells_x)
    def _(x):
        w_z[x] = 1.0 / w_z[x]

    load_hist.wait()
    wait_recv(t2[:2])
    smooth_y_halo(
        t_two, t_hy.at[1, low], t_hy.at[1, high], lower, plane_ends + plane_middle
    )
    stores = []

    def largest(x):
        hist[x] = jnp.maximum(hist[x], t_two[x] * w_z[x])

    def store_planes(start):
        pl.loop(start, start + RADIUS)(largest)
        planes = pl.ds(start, RADIUS)
        copy = pltpu.make_async_copy(
            hist.at[planes], kappa_out.at[planes], out_sem.at[1 + start // RADIUS]
        )
        copy.start()
        stores.append(copy)

    for start in range(RADIUS, cells_x - RADIUS, RADIUS):
        store_planes(start)
    wait_recv(t2[2:])
    smooth_x_halo(t_two, t_hx.at[1, low], t_hx.at[1, high], upper, row_ends + row_middle)
    for start in (0, cells_x - RADIUS):
        store_planes(start)
    nodes = (node_x, node_y, node_e, node_z, node_zx, node_ze, node_zy)
    for copy in nodes + w1 + w2 + t1 + t2 + tz + wz:
        copy.wait_send()
    for copy in [store_stress] + stores:
        copy.wait()


def finish(
    kappa_in, stress_in, labels_in, threshold, ductility, brittleness, damage_out, mises_out,
    kappa, stress, labels, damage, mises, in_sem, out_sem, *, step,
):
    cells_x = labels.shape[0]
    chunks = range(0, cells_x, step)
    pairs = ((kappa_in, kappa), (labels_in, labels), (stress_in, stress))
    loads, stores = [], []
    for i, start in enumerate(chunks):
        planes = pl.ds(start, step)
        loads.append([
            pltpu.make_async_copy(src.at[planes], dst.at[planes], in_sem.at[3 * i + k])
            for k, (src, dst) in enumerate(pairs)
        ])
        for copy in loads[-1]:
            copy.start()

    def plane(x):
        masks = phase_masks(labels[x])

        def chosen(ref):
            return jnp.where(
                masks[0], ref[0], jnp.where(masks[1], ref[1], jnp.where(masks[2], ref[2], ref[3]))
            )

        start, ductile, brittle = chosen(threshold), chosen(ductility), chosen(brittleness)
        now = kappa[x]
        grown = (
            1.0
            - start * (1.0 - ductile) / jnp.maximum(now, start)
            - ductile * jnp.exp(brittle * (start - now))
        )
        grown = jnp.where(now > start, grown, 0.0)
        damage[x] = grown
        mises[x] = (1.0 - grown) * stress[x]

    for i, start in enumerate(chunks):
        for copy in loads[i]:
            copy.wait()
        pl.loop(start, start + step)(plane)
        planes = pl.ds(start, step)
        for k, (src, dst) in enumerate(((damage, damage_out), (mises, mises_out))):
            copy = pltpu.make_async_copy(src.at[planes], dst.at[planes], out_sem.at[2 * i + k])
            copy.start()
            stores.append(copy)
    for copy in stores:
        copy.wait()


def shards(
    displacement, applied_strain, labels, history,
    modulus, poisson, threshold, ductility, brittleness, weight,
):
    cells_x, cells_y, cells_z = labels.shape
    half = cells_z // 2
    f32 = functools.partial(pltpu.VMEM, dtype=jnp.float32)
    bf16 = functools.partial(pltpu.VMEM, dtype=jnp.bfloat16)
    full = (cells_x, cells_y, cells_z)
    tile = (cells_x, cells_y, LANES)
    halo_x = f32((2, 2, RADIUS, cells_y, half))
    halo_y = f32((2, 2, cells_x, RADIUS, half))
    wide = cells_z + LANES
    copies = 29
    smem = functools.partial(pltpu.SMEM, dtype=jnp.float32)
    scratch = [
        smem(applied_strain.shape), smem(modulus.shape), smem(poisson.shape), smem(weight.shape),
        f32((3, cells_x + 1, cells_y + ROWS, wide)),
        f32((3, cells_x, ROWS, cells_z)),
        f32((3, cells_x, cells_z)),
        f32((3, cells_x, wide)),
        f32((3, ROWS, wide)),
        pltpu.VMEM(full, jnp.int32),
        f32(full), f32(full),
        f32((24, cells_z)),
        bf16((cells_z + 2 * LANES, cells_z)), bf16((cells_z + 2 * LANES, cells_z)),
        f32(full), f32(full), f32(full), f32(full), f32(full), f32(full), f32(full), f32(full),
        halo_x, halo_y, halo_x, halo_y,
        f32(tile), f32(tile), f32(tile), f32(tile),
        pltpu.SemaphoreType.DMA((8,)),
        pltpu.SemaphoreType.DMA((1 + cells_x // RADIUS,)),
        pltpu.SemaphoreType.DMA((copies,)),
        pltpu.SemaphoreType.DMA((copies,)),
    ]
    whole = pl.BlockSpec(memory_space=pl.ANY)
    scalars = pl.BlockSpec(memory_space=pltpu.SMEM)
    out = jax.ShapeDtypeStruct(full, jnp.float32)
    kappa, stress = pl.pallas_call(
        kernel,
        out_shape=(out, out),
        in_specs=[whole] * 7,
        out_specs=(whole, whole),
        scratch_shapes=scratch,
        compiler_params=pltpu.CompilerParams(
            collective_id=0, has_side_effects=True, vmem_limit_bytes=56 * 1024 * 1024
        ),
        name="strain_and_average",
    )(displacement, labels, history, applied_strain, modulus, poisson, weight)
    step = 8
    chunks = cells_x // step
    return pl.pallas_call(
        functools.partial(finish, step=step),
        out_shape=(out, out),
        in_specs=[whole] * 3 + [scalars] * 3,
        out_specs=(whole, whole),
        scratch_shapes=[
            f32(full), f32(full), pltpu.VMEM(full, jnp.int32), f32(full), f32(full),
            pltpu.SemaphoreType.DMA((3 * chunks,)),
            pltpu.SemaphoreType.DMA((2 * chunks,)),
        ],
        compiler_params=pltpu.CompilerParams(vmem_limit_bytes=56 * 1024 * 1024),
        name="damage_and_stress",
    )(kappa, stress, labels, threshold, ductility, brittleness)


def solution(mesh):
    block = P("gx", "gy", "gz")
    placed = (P(None, "gx", "gy", "gz"), P(), block, block, P(), P(), P(), P(), P(), P())
    return jax.shard_map(
        shards, mesh=mesh, in_specs=placed, out_specs=(block, block), check_vma=False
    )
```

```python
import functools
import math

import jax
import jax.numpy as jnp
from jax import lax
from jax.experimental import pallas as pl
from jax.experimental.pallas import tpu as pltpu
from jax.sharding import PartitionSpec as P

RADIUS = 8
LANES = 128
ROWS = 8
MESH = pl.DeviceIdType.MESH
TAPS = [math.exp(-2.0 * s * s / (RADIUS * RADIUS)) for s in range(RADIUS + 1)]
T_WEIGHT, T_LATERAL, T_FACTOR, T_STIFF = range(4)


def phase_masks(labels):
    return (labels == 0, labels == 1, labels == 2)


def pick(masks, tab, which):
    rows = [tab[pl.ds(4 * which + p, 1), : masks[0].shape[-1]] for p in range(4)]
    return jnp.where(
        masks[0], rows[0], jnp.where(masks[1], rows[1], jnp.where(masks[2], rows[2], rows[3]))
    )


def fill_tables(tab, modulus, poisson, weight):
    width = tab.shape[-1]

    def put(which, phase, value):
        tab[4 * which + phase : 4 * which + phase + 1, :] = value

    for p in range(4):
        wide = lambda ref: jnp.full((1, width), ref[p], jnp.float32)
        nu, w = wide(poisson), wide(weight)
        put(T_WEIGHT, p, w)
        scaled = w * (1.0 / 80.0)
        put(T_LATERAL, p, scaled * 9.0 / (1.0 - 2.0 * nu))
        put(T_FACTOR, p, scaled * scaled * 120.0 / ((1.0 + nu) * (1.0 + nu)))
        put(T_STIFF, p, wide(modulus) / (1.0 + nu) * (0.25 * math.sqrt(3.0)))


def fill_bands(band_hi, band_lo):
    depth, width = band_hi.shape

    @pl.loop(0, depth // LANES)
    def _(i):
        rows = pl.ds(pl.multiple_of(i * LANES, LANES), LANES)
        k = lax.broadcasted_iota(jnp.int32, (LANES, width), 0) + i * LANES
        n = lax.broadcasted_iota(jnp.int32, (LANES, width), 1)
        d = (k - LANES - n).astype(jnp.float32)
        g = jnp.where(jnp.abs(d) <= RADIUS, jnp.exp(d * d * (-2.0 / (RADIUS * RADIUS))), 0.0)
        hi = g.astype(jnp.bfloat16)
        band_hi[rows, :] = hi
        band_lo[rows, :] = (g - hi.astype(jnp.float32)).astype(jnp.bfloat16)


def smooth_x_own(src, dst, lanes):
    cells_x, cells_y, _ = src.shape

    @pl.loop(0, cells_y // ROWS)
    def _(j):
        rows = pl.ds(pl.multiple_of(j * ROWS, ROWS), ROWS)
        for first in range(0, cells_x, RADIUS):
            low, high = max(first - RADIUS, 0), min(first + 2 * RADIUS, cells_x)
            col = {x: src[x, rows, lanes] for x in range(low, high)}
            for x in range(first, first + RADIUS):
                total = TAPS[0] * col[x]
                for s in range(1, RADIUS + 1):
                    pair = [col[k] for k in (x - s, x + s) if k in col]
                    if pair:
                        total = total + TAPS[s] * (pair[0] + pair[1] if len(pair) > 1 else pair[0])
                dst[x, rows, lanes] = total


def ends_and_middle(count):
    return ((0, 1), (count - 1, count)), ((1, count - 1),)


def smooth_x_halo(dst, low, high, lanes, spans):
    cells_x, cells_y, _ = dst.shape

    def step(j):
        rows = pl.ds(pl.multiple_of(j * ROWS, ROWS), ROWS)
        below = [low[k, rows, :] for k in range(RADIUS)]
        above = [high[k, rows, :] for k in range(RADIUS)]
        for i in range(RADIUS):
            total = dst[i, rows, lanes]
            for k in range(i, RADIUS):
                total = total + TAPS[i + RADIUS - k] * below[k]
            dst[i, rows, lanes] = total
            x = cells_x - RADIUS + i
            total = dst[x, rows, lanes]
            for k in range(i + 1):
                total = total + TAPS[RADIUS + k - i] * above[k]
            dst[x, rows, lanes] = total

    for span in spans:
        pl.loop(*span)(step)


def smooth_rows(block):
    long = block.shape[0] - ROWS
    cells_y = block.shape[0] - 2 * RADIUS
    total = None
    for r in range(ROWS):
        part = None
        for q in range(3):
            s = ROWS * q + r
            if s > 2 * RADIUS:
                continue
            rows = cells_y if r == 0 else long
            term = TAPS[abs(s - RADIUS)] * block[ROWS * q : ROWS * q + rows]
            part = term if part is None else part + term
        if r:
            part = pltpu.roll(part, long - r, 0)[:cells_y]
        total = part if total is None else total + part
    return total


def smooth_y_own(src, dst, lanes):
    cells_x = src.shape[0]

    @pl.loop(0, cells_x // 2)
    def _(i):
        for k in range(2):
            own = src[2 * i + k, :, lanes]
            edge = jnp.zeros((RADIUS, own.shape[1]), own.dtype)
            dst[2 * i + k, :, lanes] = smooth_rows(jnp.concatenate([edge, own, edge], axis=0))


def smooth_y_halo(dst, low, high, lanes, spans):
    cells_x, cells_y, _ = dst.shape
    group = 8
    row = lax.broadcasted_iota(jnp.int32, (1, RADIUS, low.shape[2]), 1)

    def step(i):
        planes = pl.ds(i * group, group)
        below, above = low[planes], high[planes]
        first = dst[planes, 0:RADIUS, lanes]
        last = dst[planes, cells_y - RADIUS : cells_y, lanes]
        for d in range(RADIUS):
            tap = TAPS[RADIUS - d]
            if d == 0:
                first, last = first + tap * below, last + tap * above
            else:
                first = first + jnp.where(row < RADIUS - d, tap, 0.0) * pltpu.roll(
                    below, RADIUS - d, 1
                )
                last = last + jnp.where(row >= d, tap, 0.0) * pltpu.roll(above, d, 1)
        dst[planes, 0:RADIUS, lanes] = first
        dst[planes, cells_y - RADIUS : cells_y, lanes] = last

    for span in spans:
        pl.loop(*span)(step)


def banded(block, band_hi, band_lo):
    planes, cells_y, depth = block.shape
    block = block.reshape(planes * cells_y, depth)
    hi = block.astype(jnp.bfloat16)
    lo = (block - hi.astype(jnp.float32)).astype(jnp.bfloat16)
    dot = functools.partial(jnp.dot, preferred_element_type=jnp.float32)
    out = dot(lo, band_hi) + dot(hi, band_lo) + dot(hi, band_hi)
    return out.reshape(planes, cells_y, out.shape[-1])


def smooth_z_own(src, dst, band_hi, band_lo, group=8):
    own = pl.ds(LANES, src.shape[2])

    @pl.loop(0, src.shape[0] // group)
    def _(i):
        planes = pl.ds(i * group, group)
        dst[planes] = banded(src[planes], band_hi[own, :], band_lo[own, :])


def smooth_z_halo(dst, left, right, band_hi, band_lo, group=8):
    cells_z = dst.shape[2]
    first, last = pl.ds(0, LANES), pl.ds(cells_z - LANES, LANES)
    end = pl.ds(cells_z + LANES, LANES)

    @pl.loop(0, dst.shape[0] // group)
    def _(i):
        planes = pl.ds(i * group, group)
        dst[planes, :, first] += banded(left[planes], band_hi[first, first], band_lo[first, first])
        dst[planes, :, last] += banded(right[planes], band_hi[end, last], band_lo[end, last])


def kernel(
    disp, labels, history, strain0_in, modulus_in, poisson_in, weight_in,
    kappa_out, stress_out,
    strain0, modulus, poisson, weight,
    ext, sums, edge, ysend, ybuf, ebuf, lab, hist, second, tab, band_hi, band_lo,
    w_raw, w_one, w_two, w_z, t_raw, t_z, t_one, t_two,
    w_hx, w_hy, t_hx, t_hy, wl, wr, tl, tr,
    in_sem, out_sem, send_sem, recv_sem,
):
    cells_x, cells_y, cells_z = labels.shape
    half = cells_z // 2
    names = ("gx", "gy", "gz")
    count = {a: lax.axis_size(a) for a in names}
    here = {a: lax.axis_index(a) for a in names}

    def at(**moved):
        return tuple(lax.rem(here[a] + moved.get(a, 0) + count[a], count[a]) for a in names)

    x_up, x_down, y_up, y_down = at(gx=1), at(gx=-1), at(gy=1), at(gy=-1)
    z_up, z_down, d_up, d_down = at(gz=1), at(gz=-1), at(gx=1, gy=1), at(gx=-1, gy=-1)

    barrier = pltpu.get_barrier_semaphore()
    greeted = (x_up, x_down, y_up, y_down, z_up, z_down, d_up, d_down)
    for device in greeted:
        pl.semaphore_signal(barrier, inc=1, device_id=device, device_id_type=MESH)

    load_lab = pltpu.make_async_copy(labels, lab, in_sem.at[0])
    load_disp = pltpu.make_async_copy(
        disp, ext.at[:, pl.ds(0, cells_x), pl.ds(0, cells_y), pl.ds(0, cells_z)], in_sem.at[1]
    )
    scalars = ((weight_in, weight), (poisson_in, poisson), (modulus_in, modulus),
               (strain0_in, strain0))
    load_scalars = [
        pltpu.make_async_copy(src, dst, in_sem.at[2 + i]) for i, (src, dst) in enumerate(scalars)
    ]
    for copy in load_scalars:
        copy.start()
    load_edge = pltpu.make_async_copy(disp.at[:, :, pl.ds(0, ROWS)], edge, in_sem.at[6])
    load_hist = pltpu.make_async_copy(history, hist, in_sem.at[7])
    for copy in (load_edge, load_lab, load_disp, load_hist):
        copy.start()

    slots = iter(range(send_sem.shape[0]))

    def remote(src, dst, device):
        slot = next(slots)
        copy = pltpu.make_async_remote_copy(
            src_ref=src, dst_ref=dst, send_sem=send_sem.at[slot], recv_sem=recv_sem.at[slot],
            device_id=device, device_id_type=MESH,
        )
        copy.start()
        return copy

    lower, upper = pl.ds(0, half), pl.ds(half, half)
    low, high = 0, 1

    def halo_x(buf, lanes, h, phase):
        return (
            remote(buf.at[pl.ds(0, RADIUS), :, lanes], h.at[phase, high], x_down),
            remote(buf.at[pl.ds(cells_x - RADIUS, RADIUS), :, lanes], h.at[phase, low], x_up),
        )

    def halo_y(buf, lanes, h, phase):
        return (
            remote(buf.at[:, pl.ds(0, RADIUS), lanes], h.at[phase, high], y_down),
            remote(buf.at[:, pl.ds(cells_y - RADIUS, RADIUS), lanes], h.at[phase, low], y_up),
        )

    def halo_z(buf, left, right, first, size):
        planes = pl.ds(first, size)
        return (
            remote(buf.at[planes, :, pl.ds(0, LANES)], right.at[planes], z_down),
            remote(buf.at[planes, :, pl.ds(cells_z - LANES, LANES)], left.at[planes], z_up),
        )

    load_edge.wait()

    @pl.loop(0, cells_x)
    def _(x):
        for c in range(3):
            ysend[c, pl.ds(x, 1), :] = edge[c, x, 0:1, :]

    zcols = pl.ds(cells_z, LANES)
    first = pl.ds(0, LANES)
    ys = pl.ds(0, cells_y)
    pl.semaphore_wait(barrier, len(greeted))
    node_x = remote(disp.at[:, 0], ext.at[:, cells_x, ys, pl.ds(0, cells_z)], x_down)
    node_y = remote(ysend, ybuf.at[:, :, pl.ds(0, cells_z)], y_down)
    node_e = remote(disp.at[:, 0, pl.ds(0, ROWS)], ebuf.at[:, :, pl.ds(0, cells_z)], d_down)
    node_z = remote(
        disp.at[:, :, :, first], ext.at[:, pl.ds(0, cells_x), ys, zcols], z_down
    )
    for copy in load_scalars:
        copy.wait()
    fill_tables(tab, modulus, poisson, weight)
    load_lab.wait()

    @pl.loop(0, cells_x)
    def _(x):
        w_raw[x] = pick(phase_masks(lab[x]), tab, T_WEIGHT)

    w1 = halo_x(w_raw, lower, w_hx, 0) + halo_y(w_raw, upper, w_hy, 0)
    fill_bands(band_hi, band_lo)
    node_x.wait_recv()
    node_zx = remote(ext.at[:, cells_x, ys, first], ext.at[:, cells_x, ys, zcols], z_down)
    node_e.wait_recv()
    node_ze = remote(ebuf.at[:, :, first], ebuf.at[:, :, zcols], z_down)
    node_y.wait_recv()
    node_zy = remote(ybuf.at[:, :, first], ybuf.at[:, :, zcols], z_down)
    smooth_x_own(w_raw, w_one, lower)
    smooth_y_own(w_raw, w_one, upper)
    for copy in (node_z, node_zx, node_ze, node_zy):
        copy.wait_recv()

    wide = ext.shape[3]
    load_disp.wait()

    @pl.loop(0, cells_x)
    def _(x):
        for c in range(3):
            ext[c, x, cells_y : cells_y + ROWS, :] = jnp.broadcast_to(
                ybuf[c, pl.ds(x, 1), :], (ROWS, wide)
            )

    for c in range(3):
        ext[c, cells_x, cells_y : cells_y + ROWS, :] = jnp.broadcast_to(
            ebuf[c, 0:1, :], (ROWS, wide)
        )

    rows = cells_y + ROWS

    def node_sums(c, x):
        plane = ext[c, x]
        moved = pltpu.roll(plane, wide - 1, 1)[:, :cells_z]
        plane = plane[:, :cells_z]
        both, diff = moved + plane, moved - plane
        next_both = pltpu.roll(both, rows - 1, 0)[:cells_y]
        next_diff = pltpu.roll(diff, rows - 1, 0)[:cells_y]
        both, diff = both[:cells_y], diff[:cells_y]
        return both + next_both, next_both - both, diff + next_diff

    def strain_plane(x):
        gx, gy, gz = [], [], []
        for c in range(3):
            new = node_sums(c, x + 1)
            gx.append(new[0] - sums[3 * c])
            gy.append(new[1] + sums[3 * c + 1])
            gz.append(new[2] + sums[3 * c + 2])
            for k in range(3):
                sums[3 * c + k] = new[k]
        xx = 4.0 * strain0[0] + gx[0]
        yy = 4.0 * strain0[1] + gy[1]
        zz = 4.0 * strain0[2] + gz[2]
        yz = 8.0 * strain0[3] + (gy[2] + gz[1])
        xz = 8.0 * strain0[4] + (gx[2] + gz[0])
        xy = 8.0 * strain0[5] + (gx[1] + gy[0])
        trace = xx + yy + zz
        d1, d2, d3 = xx - yy, yy - zz, zz - xx
        inv = (d1 * d1 + d2 * d2 + d3 * d3) * (1.0 / 6.0) + 0.25 * (yz * yz + xz * xz + xy * xy)
        masks = phase_masks(lab[x])
        part = pick(masks, tab, T_LATERAL) * trace
        t_raw[x] = part + jnp.sqrt(part * part + pick(masks, tab, T_FACTOR) * inv)
        second[x] = inv

    for c in range(3):
        for k, value in enumerate(node_sums(c, 0)):
            sums[3 * c + k] = value

    row_ends, row_middle = ends_and_middle(cells_y // ROWS)
    plane_ends, plane_middle = ends_and_middle(cells_x // 8)

    def wait_recv(copies):
        for copy in copies:
            copy.wait_recv()

    split = cells_x // 2
    pl.loop(0, split)(strain_plane)
    tz = halo_z(t_raw, tl, tr, 0, split)
    wait_recv(w1[:2])
    smooth_x_halo(w_one, w_hx.at[0, low], w_hx.at[0, high], lower, row_ends)
    w2 = halo_y(w_one, lower, w_hy, 1)
    wait_recv(w1[2:])
    smooth_y_halo(w_one, w_hy.at[0, low], w_hy.at[0, high], upper, plane_ends)
    w2 += halo_x(w_one, upper, w_hx, 1)
    smooth_x_halo(w_one, w_hx.at[0, low], w_hx.at[0, high], lower, row_middle)
    smooth_y_halo(w_one, w_hy.at[0, low], w_hy.at[0, high], upper, plane_middle)
    pl.loop(split, cells_x)(strain_plane)
    tz += halo_z(t_raw, tl, tr, split, cells_x - split)
    smooth_z_own(t_raw, t_z, band_hi, band_lo)
    wait_recv(tz)
    smooth_z_halo(t_z, tl, tr, band_hi, band_lo)
    t1 = halo_x(t_z, lower, t_hx, 0) + halo_y(t_z, upper, t_hy, 0)
    smooth_y_own(w_one, w_two, lower)
    smooth_x_own(w_one, w_two, upper)
    wait_recv(w2)
    smooth_y_halo(w_two, w_hy.at[1, low], w_hy.at[1, high], lower, plane_ends + plane_middle)
    smooth_x_halo(w_two, w_hx.at[1, low], w_hx.at[1, high], upper, row_ends + row_middle)
    wz = halo_z(w_two, wl, wr, 0, cells_x)
    smooth_x_own(t_z, t_one, lower)
    smooth_y_own(t_z, t_one, upper)
    wait_recv(t1[:2])
    smooth_x_halo(t_one, t_hx.at[0, low], t_hx.at[0, high], lower, row_ends)
    t2 = halo_y(t_one, lower, t_hy, 1)
    wait_recv(t1[2:])
    smooth_y_halo(t_one, t_hy.at[0, low], t_hy.at[0, high], upper, plane_ends)
    t2 += halo_x(t_one, upper, t_hx, 1)
    smooth_x_halo(t_one, t_hx.at[0, low], t_hx.at[0, high], lower, row_middle)
    smooth_y_halo(t_one, t_hy.at[0, low], t_hy.at[0, high], upper, plane_middle)

    @pl.loop(0, cells_x)
    def _(x):
        second[x] = pick(phase_masks(lab[x]), tab, T_STIFF) * jnp.sqrt(second[x])

    store_stress = pltpu.make_async_copy(second, stress_out, out_sem.at[0])
    store_stress.start()
    smooth_z_own(w_two, w_z, band_hi, band_lo)
    wait_recv(wz)
    smooth_z_halo(w_z, wl, wr, band_hi, band_lo)
    smooth_y_own(t_one, t_two, lower)
    smooth_x_own(t_one, t_two, upper)

    @pl.loop(0, cells_x)
    def _(x):
        w_z[x] = 1.0 / w_z[x]

    load_hist.wait()
    wait_recv(t2[:2])
    smooth_y_halo(
        t_two, t_hy.at[1, low], t_hy.at[1, high], lower, plane_ends + plane_middle
    )
    stores = []

    def largest(x):
        hist[x] = jnp.maximum(hist[x], t_two[x] * w_z[x])

    def store_planes(start):
        pl.loop(start, start + RADIUS)(largest)
        planes = pl.ds(start, RADIUS)
        copy = pltpu.make_async_copy(
            hist.at[planes], kappa_out.at[planes], out_sem.at[1 + start // RADIUS]
        )
        copy.start()
        stores.append(copy)

    for start in range(RADIUS, cells_x - RADIUS, RADIUS):
        store_planes(start)
    wait_recv(t2[2:])
    smooth_x_halo(t_two, t_hx.at[1, low], t_hx.at[1, high], upper, row_ends + row_middle)
    for start in (0, cells_x - RADIUS):
        store_planes(start)
    nodes = (node_x, node_y, node_e, node_z, node_zx, node_ze, node_zy)
    for copy in nodes + w1 + w2 + t1 + t2 + tz + wz:
        copy.wait_send()
    for copy in [store_stress] + stores:
        copy.wait()


def finish(
    kappa_in, stress_in, labels_in, threshold, ductility, brittleness, damage_out, mises_out,
    kappa, stress, labels, damage, mises, in_sem, out_sem, *, step,
):
    cells_x = labels.shape[0]
    chunks = range(0, cells_x, step)
    pairs = ((kappa_in, kappa), (labels_in, labels), (stress_in, stress))
    loads, stores = [], []
    for i, start in enumerate(chunks):
        planes = pl.ds(start, step)
        loads.append([
            pltpu.make_async_copy(src.at[planes], dst.at[planes], in_sem.at[3 * i + k])
            for k, (src, dst) in enumerate(pairs)
        ])
        for copy in loads[-1]:
            copy.start()

    def plane(x):
        masks = phase_masks(labels[x])

        def chosen(ref):
            return jnp.where(
                masks[0], ref[0], jnp.where(masks[1], ref[1], jnp.where(masks[2], ref[2], ref[3]))
            )

        start, ductile, brittle = chosen(threshold), chosen(ductility), chosen(brittleness)
        now = kappa[x]
        grown = (
            1.0
            - start * (1.0 - ductile) / jnp.maximum(now, start)
            - ductile * jnp.exp(brittle * (start - now))
        )
        grown = jnp.where(now > start, grown, 0.0)
        damage[x] = grown
        mises[x] = (1.0 - grown) * stress[x]

    for i, start in enumerate(chunks):
        for copy in loads[i]:
            copy.wait()
        pl.loop(start, start + step)(plane)
        planes = pl.ds(start, step)
        for k, (src, dst) in enumerate(((damage, damage_out), (mises, mises_out))):
            copy = pltpu.make_async_copy(src.at[planes], dst.at[planes], out_sem.at[2 * i + k])
            copy.start()
            stores.append(copy)
    for copy in stores:
        copy.wait()


def shards(
    displacement, applied_strain, labels, history,
    modulus, poisson, threshold, ductility, brittleness, weight,
):
    cells_x, cells_y, cells_z = labels.shape
    half = cells_z // 2
    f32 = functools.partial(pltpu.VMEM, dtype=jnp.float32)
    bf16 = functools.partial(pltpu.VMEM, dtype=jnp.bfloat16)
    full = (cells_x, cells_y, cells_z)
    tile = (cells_x, cells_y, LANES)
    halo_x = f32((2, 2, RADIUS, cells_y, half))
    halo_y = f32((2, 2, cells_x, RADIUS, half))
    wide = cells_z + LANES
    copies = 29
    smem = functools.partial(pltpu.SMEM, dtype=jnp.float32)
    scratch = [
        smem(applied_strain.shape), smem(modulus.shape), smem(poisson.shape), smem(weight.shape),
        f32((3, cells_x + 1, cells_y + ROWS, wide)),
        f32((9, cells_y, cells_z)),
        f32((3, cells_x, ROWS, cells_z)),
        f32((3, cells_x, cells_z)),
        f32((3, cells_x, wide)),
        f32((3, ROWS, wide)),
        pltpu.VMEM(full, jnp.int32),
        f32(full), f32(full),
        f32((16, cells_z)),
        bf16((cells_z + 2 * LANES, cells_z)), bf16((cells_z + 2 * LANES, cells_z)),
        f32(full), f32(full), f32(full), f32(full), f32(full), f32(full), f32(full), f32(full),
        halo_x, halo_y, halo_x, halo_y,
        f32(tile), f32(tile), f32(tile), f32(tile),
        pltpu.SemaphoreType.DMA((8,)),
        pltpu.SemaphoreType.DMA((1 + cells_x // RADIUS,)),
        pltpu.SemaphoreType.DMA((copies,)),
        pltpu.SemaphoreType.DMA((copies,)),
    ]
    whole = pl.BlockSpec(memory_space=pl.ANY)
    scalars = pl.BlockSpec(memory_space=pltpu.SMEM)
    out = jax.ShapeDtypeStruct(full, jnp.float32)
    kappa, stress = pl.pallas_call(
        kernel,
        out_shape=(out, out),
        in_specs=[whole] * 7,
        out_specs=(whole, whole),
        scratch_shapes=scratch,
        compiler_params=pltpu.CompilerParams(
            collective_id=0, has_side_effects=True, vmem_limit_bytes=56 * 1024 * 1024
        ),
        name="strain_and_average",
    )(displacement, labels, history, applied_strain, modulus, poisson, weight)
    step = 8
    chunks = cells_x // step
    return pl.pallas_call(
        functools.partial(finish, step=step),
        out_shape=(out, out),
        in_specs=[whole] * 3 + [scalars] * 3,
        out_specs=(whole, whole),
        scratch_shapes=[
            f32(full), f32(full), pltpu.VMEM(full, jnp.int32), f32(full), f32(full),
            pltpu.SemaphoreType.DMA((3 * chunks,)),
            pltpu.SemaphoreType.DMA((2 * chunks,)),
        ],
        compiler_params=pltpu.CompilerParams(vmem_limit_bytes=56 * 1024 * 1024),
        name="damage_and_stress",
    )(kappa, stress, labels, threshold, ductility, brittleness)


def solution(mesh):
    block = P("gx", "gy", "gz")
    placed = (P(None, "gx", "gy", "gz"), P(), block, block, P(), P(), P(), P(), P(), P())
    return jax.shard_map(
        shards, mesh=mesh, in_specs=placed, out_specs=(block, block), check_vma=False
    )
```

```python
import functools
import math

import jax
import jax.numpy as jnp
from jax import lax
from jax.experimental import pallas as pl
from jax.experimental.pallas import tpu as pltpu
from jax.sharding import PartitionSpec as P

RADIUS = 8
LANES = 128
ROWS = 8
MESH = pl.DeviceIdType.MESH
TAPS = [math.exp(-2.0 * s * s / (RADIUS * RADIUS)) for s in range(RADIUS + 1)]
T_WEIGHT, T_LATERAL, T_FACTOR, T_STIFF = range(4)


def phase_masks(labels):
    return (labels == 0, labels == 1, labels == 2)


def pick(masks, tab, which):
    rows = [tab[pl.ds(4 * which + p, 1), : masks[0].shape[-1]] for p in range(4)]
    return jnp.where(
        masks[0], rows[0], jnp.where(masks[1], rows[1], jnp.where(masks[2], rows[2], rows[3]))
    )


def fill_tables(tab, modulus, poisson, weight):
    width = tab.shape[-1]

    def put(which, phase, value):
        tab[4 * which + phase : 4 * which + phase + 1, :] = value

    for p in range(4):
        wide = lambda ref: jnp.full((1, width), ref[p], jnp.float32)
        nu, w = wide(poisson), wide(weight)
        put(T_WEIGHT, p, w)
        scaled = w * (1.0 / 80.0)
        put(T_LATERAL, p, scaled * 9.0 / (1.0 - 2.0 * nu))
        put(T_FACTOR, p, scaled * scaled * 120.0 / ((1.0 + nu) * (1.0 + nu)))
        put(T_STIFF, p, wide(modulus) / (1.0 + nu) * (0.25 * math.sqrt(3.0)))


def fill_bands(band_hi, band_lo):
    depth, width = band_hi.shape

    @pl.loop(0, depth // LANES)
    def _(i):
        rows = pl.ds(pl.multiple_of(i * LANES, LANES), LANES)
        k = lax.broadcasted_iota(jnp.int32, (LANES, width), 0) + i * LANES
        n = lax.broadcasted_iota(jnp.int32, (LANES, width), 1)
        d = (k - LANES - n).astype(jnp.float32)
        g = jnp.where(jnp.abs(d) <= RADIUS, jnp.exp(d * d * (-2.0 / (RADIUS * RADIUS))), 0.0)
        hi = g.astype(jnp.bfloat16)
        band_hi[rows, :] = hi
        band_lo[rows, :] = (g - hi.astype(jnp.float32)).astype(jnp.bfloat16)


def smooth_x_own(src, dst, lanes):
    cells_x, cells_y, _ = src.shape

    @pl.loop(0, cells_y // ROWS)
    def _(j):
        rows = pl.ds(pl.multiple_of(j * ROWS, ROWS), ROWS)
        for first in range(0, cells_x, RADIUS):
            low, high = max(first - RADIUS, 0), min(first + 2 * RADIUS, cells_x)
            col = {x: src[x, rows, lanes] for x in range(low, high)}
            for x in range(first, first + RADIUS):
                total = TAPS[0] * col[x]
                for s in range(1, RADIUS + 1):
                    pair = [col[k] for k in (x - s, x + s) if k in col]
                    if pair:
                        total = total + TAPS[s] * (pair[0] + pair[1] if len(pair) > 1 else pair[0])
                dst[x, rows, lanes] = total


def ends_and_middle(count):
    return ((0, 1), (count - 1, count)), ((1, count - 1),)


def smooth_x_halo(dst, low, high, lanes, spans):
    cells_x, cells_y, _ = dst.shape

    def step(j):
        rows = pl.ds(pl.multiple_of(j * ROWS, ROWS), ROWS)
        below = [low[k, rows, :] for k in range(RADIUS)]
        above = [high[k, rows, :] for k in range(RADIUS)]
        for i in range(RADIUS):
            total = dst[i, rows, lanes]
            for k in range(i, RADIUS):
                total = total + TAPS[i + RADIUS - k] * below[k]
            dst[i, rows, lanes] = total
            x = cells_x - RADIUS + i
            total = dst[x, rows, lanes]
            for k in range(i + 1):
                total = total + TAPS[RADIUS + k - i] * above[k]
            dst[x, rows, lanes] = total

    for span in spans:
        pl.loop(*span)(step)


def smooth_rows(block):
    long = block.shape[0] - ROWS
    cells_y = block.shape[0] - 2 * RADIUS
    total = None
    for r in range(ROWS):
        part = None
        for q in range(3):
            s = ROWS * q + r
            if s > 2 * RADIUS:
                continue
            rows = cells_y if r == 0 else long
            term = TAPS[abs(s - RADIUS)] * block[ROWS * q : ROWS * q + rows]
            part = term if part is None else part + term
        if r:
            part = pltpu.roll(part, long - r, 0)[:cells_y]
        total = part if total is None else total + part
    return total


def smooth_y_own(src, dst, lanes):
    cells_x = src.shape[0]

    @pl.loop(0, cells_x // 2)
    def _(i):
        for k in range(2):
            own = src[2 * i + k, :, lanes]
            edge = jnp.zeros((RADIUS, own.shape[1]), own.dtype)
            dst[2 * i + k, :, lanes] = smooth_rows(jnp.concatenate([edge, own, edge], axis=0))


def smooth_y_halo(dst, low, high, lanes, spans):
    cells_x, cells_y, _ = dst.shape
    group = 8
    row = lax.broadcasted_iota(jnp.int32, (1, RADIUS, low.shape[2]), 1)

    def step(i):
        planes = pl.ds(i * group, group)
        below, above = low[planes], high[planes]
        first = dst[planes, 0:RADIUS, lanes]
        last = dst[planes, cells_y - RADIUS : cells_y, lanes]
        for d in range(RADIUS):
            tap = TAPS[RADIUS - d]
            if d == 0:
                first, last = first + tap * below, last + tap * above
            else:
                first = first + jnp.where(row < RADIUS - d, tap, 0.0) * pltpu.roll(
                    below, RADIUS - d, 1
                )
                last = last + jnp.where(row >= d, tap, 0.0) * pltpu.roll(above, d, 1)
        dst[planes, 0:RADIUS, lanes] = first
        dst[planes, cells_y - RADIUS : cells_y, lanes] = last

    for span in spans:
        pl.loop(*span)(step)


def banded(block, band_hi, band_lo):
    planes, cells_y, depth = block.shape
    block = block.reshape(planes * cells_y, depth)
    hi = block.astype(jnp.bfloat16)
    lo = (block - hi.astype(jnp.float32)).astype(jnp.bfloat16)
    dot = functools.partial(jnp.dot, preferred_element_type=jnp.float32)
    out = dot(lo, band_hi) + dot(hi, band_lo) + dot(hi, band_hi)
    return out.reshape(planes, cells_y, out.shape[-1])


def smooth_z_own(src, dst, band_hi, band_lo, group=8):
    own = pl.ds(LANES, src.shape[2])

    @pl.loop(0, src.shape[0] // group)
    def _(i):
        planes = pl.ds(i * group, group)
        dst[planes] = banded(src[planes], band_hi[own, :], band_lo[own, :])


def pack_z(src, ends):
    cells_x, cells_y, cells_z = src.shape
    per = LANES // RADIUS
    column = lax.broadcasted_iota(jnp.int32, (cells_y, LANES), 1)
    for i in range(pl.cdiv(cells_x, per)):
        tiles = [jnp.zeros((cells_y, LANES), jnp.float32)] * 2
        for p in range(min(per, cells_x - i * per)):
            x = i * per + p
            here = (column >= p * RADIUS) & (column < (p + 1) * RADIUS)
            first, last = src[x, :, 0:LANES], src[x, :, cells_z - LANES : cells_z]
            if p:
                first = pltpu.roll(first, p * RADIUS, 1)
            if p < per - 1:
                last = pltpu.roll(last, (p + 1) * RADIUS, 1)
            tiles = [jnp.where(here, first, tiles[0]), jnp.where(here, last, tiles[1])]
        ends[0, i], ends[1, i] = tiles


def smooth_z_halo(dst, left, right, band_hi, band_lo):
    cells_x, _, cells_z = dst.shape
    per = LANES // RADIUS
    first, last = pl.ds(0, LANES), pl.ds(cells_z - LANES, LANES)
    end = pl.ds(cells_z + LANES, LANES)
    group = 8
    for start in range(0, cells_x, group):
        lefts, rights = [], []
        for x in range(start, start + group):
            i, p = divmod(x, per)
            low, high = left[i], right[i]
            lefts.append(pltpu.roll(low, LANES - (p + 1) * RADIUS, 1) if p < per - 1 else low)
            rights.append(pltpu.roll(high, LANES - p * RADIUS, 1) if p else high)
        planes = pl.ds(start, group)
        dst[planes, :, first] += banded(
            jnp.stack(lefts), band_hi[first, first], band_lo[first, first]
        )
        dst[planes, :, last] += banded(jnp.stack(rights), band_hi[end, last], band_lo[end, last])


def kernel(
    disp, labels, history, strain0_in, modulus_in, poisson_in, weight_in,
    kappa_out, stress_out,
    strain0, modulus, poisson, weight,
    ext, sums, edge, ysend, ybuf, ebuf, lab, hist, second, tab, band_hi, band_lo,
    w_raw, w_one, w_two, w_z, t_raw, t_z, t_one, t_two,
    w_hx, w_hy, t_hx, t_hy, w_sx, w_sy, t_sx, t_sy, w_ends, t_ends, wl, wr, tl, tr,
    in_sem, out_sem, send_sem, recv_sem,
):
    cells_x, cells_y, cells_z = labels.shape
    half = cells_z // 2
    names = ("gx", "gy", "gz")
    count = {a: lax.axis_size(a) for a in names}
    here = {a: lax.axis_index(a) for a in names}

    def at(**moved):
        return tuple(lax.rem(here[a] + moved.get(a, 0) + count[a], count[a]) for a in names)

    x_up, x_down, y_up, y_down = at(gx=1), at(gx=-1), at(gy=1), at(gy=-1)
    z_up, z_down, d_up, d_down = at(gz=1), at(gz=-1), at(gx=1, gy=1), at(gx=-1, gy=-1)

    barrier = pltpu.get_barrier_semaphore()
    greeted = (x_up, x_down, y_up, y_down, z_up, z_down, d_up, d_down)
    for device in greeted:
        pl.semaphore_signal(barrier, inc=1, device_id=device, device_id_type=MESH)

    load_lab = pltpu.make_async_copy(labels, lab, in_sem.at[0])
    load_disp = pltpu.make_async_copy(
        disp, ext.at[:, pl.ds(0, cells_x), pl.ds(0, cells_y), pl.ds(0, cells_z)], in_sem.at[1]
    )
    scalars = ((weight_in, weight), (poisson_in, poisson), (modulus_in, modulus),
               (strain0_in, strain0))
    load_scalars = [
        pltpu.make_async_copy(src, dst, in_sem.at[2 + i]) for i, (src, dst) in enumerate(scalars)
    ]
    for copy in load_scalars:
        copy.start()
    load_edge = pltpu.make_async_copy(disp.at[:, :, pl.ds(0, ROWS)], edge, in_sem.at[6])
    load_hist = pltpu.make_async_copy(history, hist, in_sem.at[7])
    for copy in (load_edge, load_lab, load_disp, load_hist):
        copy.start()

    slots = iter(range(send_sem.shape[0]))

    def remote(src, dst, device):
        slot = next(slots)
        copy = pltpu.make_async_remote_copy(
            src_ref=src, dst_ref=dst, send_sem=send_sem.at[slot], recv_sem=recv_sem.at[slot],
            device_id=device, device_id_type=MESH,
        )
        copy.start()
        return copy

    lower, upper = pl.ds(0, half), pl.ds(half, half)
    low, high = 0, 1

    def halo_x(buf, lanes, h, phase, sent):
        sent[phase, low] = buf[0:RADIUS, :, lanes]
        down = remote(sent.at[phase, low], h.at[phase, high], x_down)
        sent[phase, high] = buf[cells_x - RADIUS : cells_x, :, lanes]
        return down, remote(sent.at[phase, high], h.at[phase, low], x_up)

    def halo_y(buf, lanes, h, phase, sent):
        sent[phase, low] = buf[:, 0:RADIUS, lanes]
        down = remote(sent.at[phase, low], h.at[phase, high], y_down)
        sent[phase, high] = buf[:, cells_y - RADIUS : cells_y, lanes]
        return down, remote(sent.at[phase, high], h.at[phase, low], y_up)

    def halo_z(buf, ends, left, right):
        pack_z(buf, ends)
        return remote(ends.at[0], right, z_down), remote(ends.at[1], left, z_up)

    load_edge.wait()

    @pl.loop(0, cells_x)
    def _(x):
        for c in range(3):
            ysend[c, pl.ds(x, 1), :] = edge[c, x, 0:1, :]

    zcols = pl.ds(cells_z, LANES)
    first = pl.ds(0, LANES)
    ys = pl.ds(0, cells_y)
    pl.semaphore_wait(barrier, len(greeted))
    node_x = remote(disp.at[:, 0], ext.at[:, cells_x, ys, pl.ds(0, cells_z)], x_down)
    node_y = remote(ysend, ybuf.at[:, :, pl.ds(0, cells_z)], y_down)
    node_e = remote(disp.at[:, 0, pl.ds(0, ROWS)], ebuf.at[:, :, pl.ds(0, cells_z)], d_down)
    node_z = remote(
        disp.at[:, :, :, first], ext.at[:, pl.ds(0, cells_x), ys, zcols], z_down
    )
    for copy in load_scalars:
        copy.wait()
    fill_tables(tab, modulus, poisson, weight)
    load_lab.wait()

    @pl.loop(0, cells_x)
    def _(x):
        w_raw[x] = pick(phase_masks(lab[x]), tab, T_WEIGHT)

    w1 = halo_x(w_raw, lower, w_hx, 0, w_sx) + halo_y(w_raw, upper, w_hy, 0, w_sy)
    fill_bands(band_hi, band_lo)
    node_x.wait_recv()
    node_zx = remote(ext.at[:, cells_x, ys, first], ext.at[:, cells_x, ys, zcols], z_down)
    node_e.wait_recv()
    node_ze = remote(ebuf.at[:, :, first], ebuf.at[:, :, zcols], z_down)
    node_y.wait_recv()
    node_zy = remote(ybuf.at[:, :, first], ybuf.at[:, :, zcols], z_down)
    smooth_x_own(w_raw, w_one, lower)
    smooth_y_own(w_raw, w_one, upper)
    for copy in (node_z, node_zx, node_ze, node_zy):
        copy.wait_recv()

    wide = ext.shape[3]
    load_disp.wait()

    @pl.loop(0, cells_x)
    def _(x):
        for c in range(3):
            ext[c, x, cells_y : cells_y + ROWS, :] = jnp.broadcast_to(
                ybuf[c, pl.ds(x, 1), :], (ROWS, wide)
            )

    for c in range(3):
        ext[c, cells_x, cells_y : cells_y + ROWS, :] = jnp.broadcast_to(
            ebuf[c, 0:1, :], (ROWS, wide)
        )

    rows = cells_y + ROWS

    def node_sums(c, x):
        plane = ext[c, x]
        moved = pltpu.roll(plane, wide - 1, 1)[:, :cells_z]
        plane = plane[:, :cells_z]
        both, diff = moved + plane, moved - plane
        next_both = pltpu.roll(both, rows - 1, 0)[:cells_y]
        next_diff = pltpu.roll(diff, rows - 1, 0)[:cells_y]
        both, diff = both[:cells_y], diff[:cells_y]
        return both + next_both, next_both - both, diff + next_diff

    def strain_plane(x):
        gx, gy, gz = [], [], []
        for c in range(3):
            new = node_sums(c, x + 1)
            gx.append(new[0] - sums[3 * c])
            gy.append(new[1] + sums[3 * c + 1])
            gz.append(new[2] + sums[3 * c + 2])
            for k in range(3):
                sums[3 * c + k] = new[k]
        xx = 4.0 * strain0[0] + gx[0]
        yy = 4.0 * strain0[1] + gy[1]
        zz = 4.0 * strain0[2] + gz[2]
        yz = 8.0 * strain0[3] + (gy[2] + gz[1])
        xz = 8.0 * strain0[4] + (gx[2] + gz[0])
        xy = 8.0 * strain0[5] + (gx[1] + gy[0])
        trace = xx + yy + zz
        d1, d2, d3 = xx - yy, yy - zz, zz - xx
        inv = (d1 * d1 + d2 * d2 + d3 * d3) * (1.0 / 6.0) + 0.25 * (yz * yz + xz * xz + xy * xy)
        masks = phase_masks(lab[x])
        part = pick(masks, tab, T_LATERAL) * trace
        t_raw[x] = part + jnp.sqrt(part * part + pick(masks, tab, T_FACTOR) * inv)
        second[x] = inv

    for c in range(3):
        for k, value in enumerate(node_sums(c, 0)):
            sums[3 * c + k] = value

    row_ends, row_middle = ends_and_middle(cells_y // ROWS)
    plane_ends, plane_middle = ends_and_middle(cells_x // 8)

    def wait_recv(copies):
        for copy in copies:
            copy.wait_recv()

    split = 3 * cells_x // 8
    pl.loop(0, split)(strain_plane)
    wait_recv(w1[:2])
    smooth_x_halo(w_one, w_hx.at[0, low], w_hx.at[0, high], lower, row_ends)
    w2 = halo_y(w_one, lower, w_hy, 1, w_sy)
    wait_recv(w1[2:])
    smooth_y_halo(w_one, w_hy.at[0, low], w_hy.at[0, high], upper, plane_ends)
    w2 += halo_x(w_one, upper, w_hx, 1, w_sx)
    smooth_x_halo(w_one, w_hx.at[0, low], w_hx.at[0, high], lower, row_middle)
    smooth_y_halo(w_one, w_hy.at[0, low], w_hy.at[0, high], upper, plane_middle)
    pl.loop(split, cells_x)(strain_plane)
    tz = halo_z(t_raw, t_ends, tl, tr)
    smooth_z_own(t_raw, t_z, band_hi, band_lo)
    wait_recv(tz)
    smooth_z_halo(t_z, tl, tr, band_hi, band_lo)
    t1 = halo_x(t_z, lower, t_hx, 0, t_sx) + halo_y(t_z, upper, t_hy, 0, t_sy)
    smooth_y_own(w_one, w_two, lower)
    smooth_x_own(w_one, w_two, upper)
    wait_recv(w2)
    smooth_y_halo(w_two, w_hy.at[1, low], w_hy.at[1, high], lower, plane_ends + plane_middle)
    smooth_x_halo(w_two, w_hx.at[1, low], w_hx.at[1, high], upper, row_ends + row_middle)
    wz = halo_z(w_two, w_ends, wl, wr)
    smooth_x_own(t_z, t_one, lower)
    smooth_y_own(t_z, t_one, upper)
    wait_recv(t1[:2])
    smooth_x_halo(t_one, t_hx.at[0, low], t_hx.at[0, high], lower, row_ends)
    t2 = halo_y(t_one, lower, t_hy, 1, t_sy)
    wait_recv(t1[2:])
    smooth_y_halo(t_one, t_hy.at[0, low], t_hy.at[0, high], upper, plane_ends)
    t2 += halo_x(t_one, upper, t_hx, 1, t_sx)
    smooth_x_halo(t_one, t_hx.at[0, low], t_hx.at[0, high], lower, row_middle)
    smooth_y_halo(t_one, t_hy.at[0, low], t_hy.at[0, high], upper, plane_middle)

    @pl.loop(0, cells_x)
    def _(x):
        second[x] = pick(phase_masks(lab[x]), tab, T_STIFF) * jnp.sqrt(second[x])

    store_stress = pltpu.make_async_copy(second, stress_out, out_sem.at[0])
    store_stress.start()
    smooth_z_own(w_two, w_z, band_hi, band_lo)
    wait_recv(wz)
    smooth_z_halo(w_z, wl, wr, band_hi, band_lo)
    smooth_y_own(t_one, t_two, lower)
    smooth_x_own(t_one, t_two, upper)

    @pl.loop(0, cells_x)
    def _(x):
        w_z[x] = 1.0 / w_z[x]

    load_hist.wait()
    wait_recv(t2[:2])
    smooth_y_halo(
        t_two, t_hy.at[1, low], t_hy.at[1, high], lower, plane_ends + plane_middle
    )
    stores = []

    def largest(x):
        hist[x] = jnp.maximum(hist[x], t_two[x] * w_z[x])

    def store_planes(start):
        pl.loop(start, start + RADIUS)(largest)
        planes = pl.ds(start, RADIUS)
        copy = pltpu.make_async_copy(
            hist.at[planes], kappa_out.at[planes], out_sem.at[1 + start // RADIUS]
        )
        copy.start()
        stores.append(copy)

    for start in range(RADIUS, cells_x - RADIUS, RADIUS):
        store_planes(start)
    wait_recv(t2[2:])
    smooth_x_halo(t_two, t_hx.at[1, low], t_hx.at[1, high], upper, row_ends + row_middle)
    for start in (0, cells_x - RADIUS):
        store_planes(start)
    nodes = (node_x, node_y, node_e, node_z, node_zx, node_ze, node_zy)
    for copy in nodes + w1 + w2 + t1 + t2 + tz + wz:
        copy.wait_send()
    for copy in [store_stress] + stores:
        copy.wait()


def finish(
    kappa_in, stress_in, labels_in, threshold, ductility, brittleness, damage_out, mises_out,
    kappa, stress, labels, damage, mises, in_sem, out_sem, *, step,
):
    cells_x = labels.shape[0]
    chunks = range(0, cells_x, step)
    pairs = ((kappa_in, kappa), (labels_in, labels), (stress_in, stress))
    loads, stores = [], []
    for i, start in enumerate(chunks):
        planes = pl.ds(start, step)
        loads.append([
            pltpu.make_async_copy(src.at[planes], dst.at[planes], in_sem.at[3 * i + k])
            for k, (src, dst) in enumerate(pairs)
        ])
        for copy in loads[-1]:
            copy.start()

    def plane(x):
        masks = phase_masks(labels[x])

        def chosen(ref):
            return jnp.where(
                masks[0], ref[0], jnp.where(masks[1], ref[1], jnp.where(masks[2], ref[2], ref[3]))
            )

        start, ductile, brittle = chosen(threshold), chosen(ductility), chosen(brittleness)
        now = kappa[x]
        grown = (
            1.0
            - start * (1.0 - ductile) / jnp.maximum(now, start)
            - ductile * jnp.exp(brittle * (start - now))
        )
        grown = jnp.where(now > start, grown, 0.0)
        damage[x] = grown
        mises[x] = (1.0 - grown) * stress[x]

    for i, start in enumerate(chunks):
        for copy in loads[i]:
            copy.wait()
        pl.loop(start, start + step)(plane)
        planes = pl.ds(start, step)
        for k, (src, dst) in enumerate(((damage, damage_out), (mises, mises_out))):
            copy = pltpu.make_async_copy(src.at[planes], dst.at[planes], out_sem.at[2 * i + k])
            copy.start()
            stores.append(copy)
    for copy in stores:
        copy.wait()


def shards(
    displacement, applied_strain, labels, history,
    modulus, poisson, threshold, ductility, brittleness, weight,
):
    cells_x, cells_y, cells_z = labels.shape
    half = cells_z // 2
    f32 = functools.partial(pltpu.VMEM, dtype=jnp.float32)
    bf16 = functools.partial(pltpu.VMEM, dtype=jnp.bfloat16)
    full = (cells_x, cells_y, cells_z)
    tile = (pl.cdiv(cells_x * RADIUS, LANES), cells_y, LANES)
    halo_x = f32((2, 2, RADIUS, cells_y, half))
    halo_y = f32((2, 2, cells_x, RADIUS, half))
    wide = cells_z + LANES
    copies = 27
    smem = functools.partial(pltpu.SMEM, dtype=jnp.float32)
    scratch = [
        smem(applied_strain.shape), smem(modulus.shape), smem(poisson.shape), smem(weight.shape),
        f32((3, cells_x + 1, cells_y + ROWS, wide)),
        f32((9, cells_y, cells_z)),
        f32((3, cells_x, ROWS, cells_z)),
        f32((3, cells_x, cells_z)),
        f32((3, cells_x, wide)),
        f32((3, ROWS, wide)),
        pltpu.VMEM(full, jnp.int32),
        f32(full), f32(full),
        f32((16, cells_z)),
        bf16((cells_z + 2 * LANES, cells_z)), bf16((cells_z + 2 * LANES, cells_z)),
        f32(full), f32(full), f32(full), f32(full), f32(full), f32(full), f32(full), f32(full),
        halo_x, halo_y, halo_x, halo_y, halo_x, halo_y, halo_x, halo_y,
        f32((2,) + tile), f32((2,) + tile),
        f32(tile), f32(tile), f32(tile), f32(tile),
        pltpu.SemaphoreType.DMA((8,)),
        pltpu.SemaphoreType.DMA((1 + cells_x // RADIUS,)),
        pltpu.SemaphoreType.DMA((copies,)),
        pltpu.SemaphoreType.DMA((copies,)),
    ]
    whole = pl.BlockSpec(memory_space=pl.ANY)
    scalars = pl.BlockSpec(memory_space=pltpu.SMEM)
    out = jax.ShapeDtypeStruct(full, jnp.float32)
    kappa, stress = pl.pallas_call(
        kernel,
        out_shape=(out, out),
        in_specs=[whole] * 7,
        out_specs=(whole, whole),
        scratch_shapes=scratch,
        compiler_params=pltpu.CompilerParams(
            collective_id=0, has_side_effects=True, vmem_limit_bytes=56 * 1024 * 1024
        ),
        name="strain_and_average",
    )(displacement, labels, history, applied_strain, modulus, poisson, weight)
    step = 8
    chunks = cells_x // step
    return pl.pallas_call(
        functools.partial(finish, step=step),
        out_shape=(out, out),
        in_specs=[whole] * 3 + [scalars] * 3,
        out_specs=(whole, whole),
        scratch_shapes=[
            f32(full), f32(full), pltpu.VMEM(full, jnp.int32), f32(full), f32(full),
            pltpu.SemaphoreType.DMA((3 * chunks,)),
            pltpu.SemaphoreType.DMA((2 * chunks,)),
        ],
        compiler_params=pltpu.CompilerParams(vmem_limit_bytes=56 * 1024 * 1024),
        name="damage_and_stress",
    )(kappa, stress, labels, threshold, ductility, brittleness)


def solution(mesh):
    block = P("gx", "gy", "gz")
    placed = (P(None, "gx", "gy", "gz"), P(), block, block, P(), P(), P(), P(), P(), P())
    return jax.shard_map(
        shards, mesh=mesh, in_specs=placed, out_specs=(block, block), check_vma=False
    )
```

```python
import functools
import math

import jax
import jax.numpy as jnp
from jax import lax
from jax.experimental import pallas as pl
from jax.experimental.pallas import tpu as pltpu
from jax.sharding import PartitionSpec as P

RADIUS = 8
LANES = 128
ROWS = 8
MESH = pl.DeviceIdType.MESH
TAPS = [math.exp(-2.0 * s * s / (RADIUS * RADIUS)) for s in range(RADIUS + 1)]
T_WEIGHT, T_LATERAL, T_FACTOR, T_STIFF = range(4)


def phase_masks(labels):
    return (labels == 0, labels == 1, labels == 2)


def pick(masks, tab, which):
    rows = [tab[pl.ds(4 * which + p, 1), : masks[0].shape[-1]] for p in range(4)]
    return jnp.where(
        masks[0], rows[0], jnp.where(masks[1], rows[1], jnp.where(masks[2], rows[2], rows[3]))
    )


def fill_tables(tab, modulus, poisson, weight):
    width = tab.shape[-1]

    def put(which, phase, value):
        tab[4 * which + phase : 4 * which + phase + 1, :] = value

    for p in range(4):
        wide = lambda ref: jnp.full((1, width), ref[p], jnp.float32)
        nu, w = wide(poisson), wide(weight)
        put(T_WEIGHT, p, w)
        scaled = w * (1.0 / 80.0)
        put(T_LATERAL, p, scaled * 9.0 / (1.0 - 2.0 * nu))
        put(T_FACTOR, p, scaled * scaled * 120.0 / ((1.0 + nu) * (1.0 + nu)))
        put(T_STIFF, p, wide(modulus) / (1.0 + nu) * (0.25 * math.sqrt(3.0)))


def fill_bands(band_hi, band_lo):
    depth, width = band_hi.shape

    @pl.loop(0, depth // LANES)
    def _(i):
        rows = pl.ds(pl.multiple_of(i * LANES, LANES), LANES)
        k = lax.broadcasted_iota(jnp.int32, (LANES, width), 0) + i * LANES
        n = lax.broadcasted_iota(jnp.int32, (LANES, width), 1)
        d = (k - LANES - n).astype(jnp.float32)
        g = jnp.where(jnp.abs(d) <= RADIUS, jnp.exp(d * d * (-2.0 / (RADIUS * RADIUS))), 0.0)
        hi = g.astype(jnp.bfloat16)
        band_hi[rows, :] = hi
        band_lo[rows, :] = (g - hi.astype(jnp.float32)).astype(jnp.bfloat16)


def smooth_x_own(src, dst, lanes):
    cells_x, cells_y, _ = src.shape

    @pl.loop(0, cells_y // ROWS)
    def _(j):
        rows = pl.ds(pl.multiple_of(j * ROWS, ROWS), ROWS)
        for first in range(0, cells_x, RADIUS):
            low, high = max(first - RADIUS, 0), min(first + 2 * RADIUS, cells_x)
            col = {x: src[x, rows, lanes] for x in range(low, high)}
            for x in range(first, first + RADIUS):
                total = TAPS[0] * col[x]
                for s in range(1, RADIUS + 1):
                    pair = [col[k] for k in (x - s, x + s) if k in col]
                    if pair:
                        total = total + TAPS[s] * (pair[0] + pair[1] if len(pair) > 1 else pair[0])
                dst[x, rows, lanes] = total


def ends_and_middle(count):
    return ((0, 1, 0), (count - 1, count, 2 - count)), ((1, count - 1, 1),)


def smooth_x_halo(dst, low, high, lanes, spans):
    cells_x, cells_y, _ = dst.shape

    def step(j, offset):
        rows = pl.ds(pl.multiple_of(j * ROWS, ROWS), ROWS)
        held = pl.ds(pl.multiple_of((j + offset) * ROWS, ROWS), ROWS)
        below = [low[k, held, :] for k in range(RADIUS)]
        above = [high[k, held, :] for k in range(RADIUS)]
        for i in range(RADIUS):
            total = dst[i, rows, lanes]
            for k in range(i, RADIUS):
                total = total + TAPS[i + RADIUS - k] * below[k]
            dst[i, rows, lanes] = total
            x = cells_x - RADIUS + i
            total = dst[x, rows, lanes]
            for k in range(i + 1):
                total = total + TAPS[RADIUS + k - i] * above[k]
            dst[x, rows, lanes] = total

    for start, stop, offset in spans:
        pl.loop(start, stop)(functools.partial(step, offset=offset))


def smooth_rows(block):
    long = block.shape[0] - ROWS
    cells_y = block.shape[0] - 2 * RADIUS
    total = None
    for r in range(ROWS):
        part = None
        for q in range(3):
            s = ROWS * q + r
            if s > 2 * RADIUS:
                continue
            rows = cells_y if r == 0 else long
            term = TAPS[abs(s - RADIUS)] * block[ROWS * q : ROWS * q + rows]
            part = term if part is None else part + term
        if r:
            part = pltpu.roll(part, long - r, 0)[:cells_y]
        total = part if total is None else total + part
    return total


def smooth_y_own(src, dst, lanes):
    cells_x = src.shape[0]

    @pl.loop(0, cells_x // 2)
    def _(i):
        for k in range(2):
            own = src[2 * i + k, :, lanes]
            edge = jnp.zeros((RADIUS, own.shape[1]), own.dtype)
            dst[2 * i + k, :, lanes] = smooth_rows(jnp.concatenate([edge, own, edge], axis=0))


def smooth_y_halo(dst, low, high, lanes, spans):
    cells_x, cells_y, _ = dst.shape
    group = 8
    row = lax.broadcasted_iota(jnp.int32, (1, RADIUS, low.shape[2]), 1)

    def step(i, offset):
        planes = pl.ds(i * group, group)
        held = pl.ds((i + offset) * group, group)
        below, above = low[held], high[held]
        first = dst[planes, 0:RADIUS, lanes]
        last = dst[planes, cells_y - RADIUS : cells_y, lanes]
        for d in range(RADIUS):
            tap = TAPS[RADIUS - d]
            if d == 0:
                first, last = first + tap * below, last + tap * above
            else:
                first = first + jnp.where(row < RADIUS - d, tap, 0.0) * pltpu.roll(
                    below, RADIUS - d, 1
                )
                last = last + jnp.where(row >= d, tap, 0.0) * pltpu.roll(above, d, 1)
        dst[planes, 0:RADIUS, lanes] = first
        dst[planes, cells_y - RADIUS : cells_y, lanes] = last

    for start, stop, offset in spans:
        pl.loop(start, stop)(functools.partial(step, offset=offset))


def banded(block, band_hi, band_lo):
    planes, cells_y, depth = block.shape
    block = block.reshape(planes * cells_y, depth)
    hi = block.astype(jnp.bfloat16)
    lo = (block - hi.astype(jnp.float32)).astype(jnp.bfloat16)
    dot = functools.partial(jnp.dot, preferred_element_type=jnp.float32)
    out = dot(lo, band_hi) + dot(hi, band_lo) + dot(hi, band_hi)
    return out.reshape(planes, cells_y, out.shape[-1])


def smooth_z_own(src, dst, band_hi, band_lo, group=8):
    own = pl.ds(LANES, src.shape[2])

    @pl.loop(0, src.shape[0] // group)
    def _(i):
        planes = pl.ds(i * group, group)
        dst[planes] = banded(src[planes], band_hi[own, :], band_lo[own, :])


def pack_z(src, ends):
    cells_x, cells_y, cells_z = src.shape
    per = LANES // RADIUS
    column = lax.broadcasted_iota(jnp.int32, (cells_y, LANES), 1)
    for i in range(pl.cdiv(cells_x, per)):
        tiles = [jnp.zeros((cells_y, LANES), jnp.float32)] * 2
        for p in range(min(per, cells_x - i * per)):
            x = i * per + p
            here = (column >= p * RADIUS) & (column < (p + 1) * RADIUS)
            first, last = src[x, :, 0:LANES], src[x, :, cells_z - LANES : cells_z]
            if p:
                first = pltpu.roll(first, p * RADIUS, 1)
            if p < per - 1:
                last = pltpu.roll(last, (p + 1) * RADIUS, 1)
            tiles = [jnp.where(here, first, tiles[0]), jnp.where(here, last, tiles[1])]
        ends[0, i], ends[1, i] = tiles


def smooth_z_halo(dst, left, right, band_hi, band_lo):
    cells_x, _, cells_z = dst.shape
    per = LANES // RADIUS
    first, last = pl.ds(0, LANES), pl.ds(cells_z - LANES, LANES)
    end = pl.ds(cells_z + LANES, LANES)
    group = 8
    for start in range(0, cells_x, group):
        lefts, rights = [], []
        for x in range(start, start + group):
            i, p = divmod(x, per)
            low, high = left[i], right[i]
            lefts.append(pltpu.roll(low, LANES - (p + 1) * RADIUS, 1) if p < per - 1 else low)
            rights.append(pltpu.roll(high, LANES - p * RADIUS, 1) if p else high)
        planes = pl.ds(start, group)
        dst[planes, :, first] += banded(
            jnp.stack(lefts), band_hi[first, first], band_lo[first, first]
        )
        dst[planes, :, last] += banded(jnp.stack(rights), band_hi[end, last], band_lo[end, last])


def kernel(
    disp, labels, history, strain0_in, modulus_in, poisson_in, weight_in,
    kappa_out, stress_out,
    strain0, modulus, poisson, weight,
    ext, sums, edge, ysend, ybuf, ebuf, lab, hist, second, tab, band_hi, band_lo,
    w_raw, w_one, w_two, w_z, t_raw, t_z, t_one, t_two,
    w_hx, w_hy, t_hx, t_hy, w_sx, w_sy, t_sx, t_sy, w_ends, t_ends, wl, wr, tl, tr,
    in_sem, out_sem, send_sem, recv_sem,
):
    cells_x, cells_y, cells_z = labels.shape
    half = cells_z // 2
    names = ("gx", "gy", "gz")
    count = {a: lax.axis_size(a) for a in names}
    here = {a: lax.axis_index(a) for a in names}

    def at(**moved):
        return tuple(lax.rem(here[a] + moved.get(a, 0) + count[a], count[a]) for a in names)

    x_up, x_down, y_up, y_down = at(gx=1), at(gx=-1), at(gy=1), at(gy=-1)
    z_up, z_down, d_up, d_down = at(gz=1), at(gz=-1), at(gx=1, gy=1), at(gx=-1, gy=-1)

    barrier = pltpu.get_barrier_semaphore()
    greeted = (x_up, x_down, y_up, y_down, z_up, z_down, d_up, d_down)
    for device in greeted:
        pl.semaphore_signal(barrier, inc=1, device_id=device, device_id_type=MESH)

    load_lab = pltpu.make_async_copy(labels, lab, in_sem.at[0])
    load_disp = pltpu.make_async_copy(
        disp, ext.at[:, pl.ds(0, cells_x), pl.ds(0, cells_y), pl.ds(0, cells_z)], in_sem.at[1]
    )
    scalars = ((weight_in, weight), (poisson_in, poisson), (modulus_in, modulus),
               (strain0_in, strain0))
    load_scalars = [
        pltpu.make_async_copy(src, dst, in_sem.at[2 + i]) for i, (src, dst) in enumerate(scalars)
    ]
    for copy in load_scalars:
        copy.start()
    load_edge = pltpu.make_async_copy(disp.at[:, :, pl.ds(0, ROWS)], edge, in_sem.at[6])
    load_hist = pltpu.make_async_copy(history, hist, in_sem.at[7])
    for copy in (load_edge, load_lab, load_disp, load_hist):
        copy.start()

    slots = iter(range(send_sem.shape[0]))

    def remote(src, dst, device):
        slot = next(slots)
        copy = pltpu.make_async_remote_copy(
            src_ref=src, dst_ref=dst, send_sem=send_sem.at[slot], recv_sem=recv_sem.at[slot],
            device_id=device, device_id_type=MESH,
        )
        copy.start()
        return copy

    lower, upper = pl.ds(0, half), pl.ds(half, half)
    low, high = 0, 1

    row_ends, row_middle = ends_and_middle(cells_y // ROWS)
    plane_ends, plane_middle = ends_and_middle(cells_x // 8)

    def wait_recv(copies):
        for copy in copies:
            copy.wait_recv()

    ends_first = lambda size: (
        (pl.ds(0, RADIUS), pl.ds(0, RADIUS)),
        (pl.ds(RADIUS, RADIUS), pl.ds(size - RADIUS, RADIUS)),
        (pl.ds(2 * RADIUS, size - 2 * RADIUS), pl.ds(RADIUS, size - 2 * RADIUS)),
    )

    def halo_x(buf, lanes, h, phase, sent, rest):
        for to, of in ends_first(cells_y)[2:] if rest else ends_first(cells_y)[:2]:
            sent[phase, low, :, to, :] = buf[0:RADIUS, of, lanes]
            sent[phase, high, :, to, :] = buf[cells_x - RADIUS : cells_x, of, lanes]
        part = pl.ds(2 * RADIUS, cells_y - 2 * RADIUS) if rest else pl.ds(0, 2 * RADIUS)
        return (
            remote(sent.at[phase, low, :, part], h.at[phase, high, :, part], x_down),
            remote(sent.at[phase, high, :, part], h.at[phase, low, :, part], x_up),
        )

    def halo_y(buf, lanes, h, phase, sent, rest):
        for to, of in ends_first(cells_x)[2:] if rest else ends_first(cells_x)[:2]:
            sent[phase, low, to] = buf[of, 0:RADIUS, lanes]
            sent[phase, high, to] = buf[of, cells_y - RADIUS : cells_y, lanes]
        part = pl.ds(2 * RADIUS, cells_x - 2 * RADIUS) if rest else pl.ds(0, 2 * RADIUS)
        return (
            remote(sent.at[phase, low, part], h.at[phase, high, part], y_down),
            remote(sent.at[phase, high, part], h.at[phase, low, part], y_up),
        )

    def first_halos(buf, hx, hy, sx, sy):
        sent = ()
        for rest in (False, True):
            sent += halo_x(buf, lower, hx, 0, sx, rest) + halo_y(buf, upper, hy, 0, sy, rest)
        return sent

    def second_halos(one, first, hx, hy, sx, sy):
        from_x, from_y = (hx.at[0, low], hx.at[0, high]), (hy.at[0, low], hy.at[0, high])
        wait_recv(first[0:2])
        smooth_x_halo(one, *from_x, lower, row_ends)
        along_y = halo_y(one, lower, hy, 1, sy, False) + halo_y(one, lower, hy, 1, sy, True)
        wait_recv(first[2:4])
        smooth_y_halo(one, *from_y, upper, plane_ends)
        along_x = halo_x(one, upper, hx, 1, sx, False) + halo_x(one, upper, hx, 1, sx, True)
        wait_recv(first[4:6])
        smooth_x_halo(one, *from_x, lower, row_middle)
        wait_recv(first[6:8])
        smooth_y_halo(one, *from_y, upper, plane_middle)
        return along_y + along_x

    def halo_z(buf, ends, left, right):
        pack_z(buf, ends)
        return remote(ends.at[0], right, z_down), remote(ends.at[1], left, z_up)

    load_edge.wait()

    @pl.loop(0, cells_x)
    def _(x):
        for c in range(3):
            ysend[c, pl.ds(x, 1), :] = edge[c, x, 0:1, :]

    zcols = pl.ds(cells_z, LANES)
    first = pl.ds(0, LANES)
    ys = pl.ds(0, cells_y)
    pl.semaphore_wait(barrier, len(greeted))
    node_x = remote(disp.at[:, 0], ext.at[:, cells_x, ys, pl.ds(0, cells_z)], x_down)
    node_y = remote(ysend, ybuf.at[:, :, pl.ds(0, cells_z)], y_down)
    node_e = remote(disp.at[:, 0, pl.ds(0, ROWS)], ebuf.at[:, :, pl.ds(0, cells_z)], d_down)
    node_z = remote(
        disp.at[:, :, :, first], ext.at[:, pl.ds(0, cells_x), ys, zcols], z_down
    )
    for copy in load_scalars:
        copy.wait()
    fill_tables(tab, modulus, poisson, weight)
    load_lab.wait()

    @pl.loop(0, cells_x)
    def _(x):
        w_raw[x] = pick(phase_masks(lab[x]), tab, T_WEIGHT)

    w1 = first_halos(w_raw, w_hx, w_hy, w_sx, w_sy)
    fill_bands(band_hi, band_lo)
    node_x.wait_recv()
    node_zx = remote(ext.at[:, cells_x, ys, first], ext.at[:, cells_x, ys, zcols], z_down)
    node_e.wait_recv()
    node_ze = remote(ebuf.at[:, :, first], ebuf.at[:, :, zcols], z_down)
    node_y.wait_recv()
    node_zy = remote(ybuf.at[:, :, first], ybuf.at[:, :, zcols], z_down)
    smooth_x_own(w_raw, w_one, lower)
    smooth_y_own(w_raw, w_one, upper)
    for copy in (node_z, node_zx, node_ze, node_zy):
        copy.wait_recv()

    wide = ext.shape[3]
    load_disp.wait()

    @pl.loop(0, cells_x)
    def _(x):
        for c in range(3):
            ext[c, x, cells_y : cells_y + ROWS, :] = jnp.broadcast_to(
                ybuf[c, pl.ds(x, 1), :], (ROWS, wide)
            )

    for c in range(3):
        ext[c, cells_x, cells_y : cells_y + ROWS, :] = jnp.broadcast_to(
            ebuf[c, 0:1, :], (ROWS, wide)
        )

    rows = cells_y + ROWS

    def node_sums(c, x):
        plane = ext[c, x]
        moved = pltpu.roll(plane, wide - 1, 1)[:, :cells_z]
        plane = plane[:, :cells_z]
        both, diff = moved + plane, moved - plane
        next_both = pltpu.roll(both, rows - 1, 0)[:cells_y]
        next_diff = pltpu.roll(diff, rows - 1, 0)[:cells_y]
        both, diff = both[:cells_y], diff[:cells_y]
        return both + next_both, next_both - both, diff + next_diff

    def strain_plane(x):
        gx, gy, gz = [], [], []
        for c in range(3):
            new = node_sums(c, x + 1)
            gx.append(new[0] - sums[3 * c])
            gy.append(new[1] + sums[3 * c + 1])
            gz.append(new[2] + sums[3 * c + 2])
            for k in range(3):
                sums[3 * c + k] = new[k]
        xx = 4.0 * strain0[0] + gx[0]
        yy = 4.0 * strain0[1] + gy[1]
        zz = 4.0 * strain0[2] + gz[2]
        yz = 8.0 * strain0[3] + (gy[2] + gz[1])
        xz = 8.0 * strain0[4] + (gx[2] + gz[0])
        xy = 8.0 * strain0[5] + (gx[1] + gy[0])
        trace = xx + yy + zz
        d1, d2, d3 = xx - yy, yy - zz, zz - xx
        inv = (d1 * d1 + d2 * d2 + d3 * d3) * (1.0 / 6.0) + 0.25 * (yz * yz + xz * xz + xy * xy)
        masks = phase_masks(lab[x])
        part = pick(masks, tab, T_LATERAL) * trace
        t_raw[x] = part + jnp.sqrt(part * part + pick(masks, tab, T_FACTOR) * inv)
        second[x] = inv

    for c in range(3):
        for k, value in enumerate(node_sums(c, 0)):
            sums[3 * c + k] = value

    split = 3 * cells_x // 8
    pl.loop(0, split)(strain_plane)
    w2 = second_halos(w_one, w1, w_hx, w_hy, w_sx, w_sy)
    pl.loop(split, cells_x)(strain_plane)
    tz = halo_z(t_raw, t_ends, tl, tr)
    smooth_z_own(t_raw, t_z, band_hi, band_lo)
    wait_recv(tz)
    smooth_z_halo(t_z, tl, tr, band_hi, band_lo)
    t1 = first_halos(t_z, t_hx, t_hy, t_sx, t_sy)
    smooth_y_own(w_one, w_two, lower)
    smooth_x_own(w_one, w_two, upper)
    wait_recv(w2)
    smooth_y_halo(w_two, w_hy.at[1, low], w_hy.at[1, high], lower, plane_ends + plane_middle)
    smooth_x_halo(w_two, w_hx.at[1, low], w_hx.at[1, high], upper, row_ends + row_middle)
    wz = halo_z(w_two, w_ends, wl, wr)
    smooth_x_own(t_z, t_one, lower)
    smooth_y_own(t_z, t_one, upper)
    t2 = second_halos(t_one, t1, t_hx, t_hy, t_sx, t_sy)

    @pl.loop(0, cells_x)
    def _(x):
        second[x] = pick(phase_masks(lab[x]), tab, T_STIFF) * jnp.sqrt(second[x])

    store_stress = pltpu.make_async_copy(second, stress_out, out_sem.at[0])
    store_stress.start()
    smooth_z_own(w_two, w_z, band_hi, band_lo)
    wait_recv(wz)
    smooth_z_halo(w_z, wl, wr, band_hi, band_lo)
    smooth_y_own(t_one, t_two, lower)
    smooth_x_own(t_one, t_two, upper)

    @pl.loop(0, cells_x)
    def _(x):
        w_z[x] = 1.0 / w_z[x]

    load_hist.wait()
    wait_recv(t2[:4])
    smooth_y_halo(
        t_two, t_hy.at[1, low], t_hy.at[1, high], lower, plane_ends + plane_middle
    )
    stores = []

    def largest(x):
        hist[x] = jnp.maximum(hist[x], t_two[x] * w_z[x])

    def store_planes(start):
        pl.loop(start, start + RADIUS)(largest)
        planes = pl.ds(start, RADIUS)
        copy = pltpu.make_async_copy(
            hist.at[planes], kappa_out.at[planes], out_sem.at[1 + start // RADIUS]
        )
        copy.start()
        stores.append(copy)

    for start in range(RADIUS, cells_x - RADIUS, RADIUS):
        store_planes(start)
    wait_recv(t2[4:])
    smooth_x_halo(t_two, t_hx.at[1, low], t_hx.at[1, high], upper, row_ends + row_middle)
    for start in (0, cells_x - RADIUS):
        store_planes(start)
    nodes = (node_x, node_y, node_e, node_z, node_zx, node_ze, node_zy)
    for copy in nodes + w1 + w2 + t1 + t2 + tz + wz:
        copy.wait_send()
    for copy in [store_stress] + stores:
        copy.wait()


def finish(
    kappa_in, stress_in, labels_in, threshold, ductility, brittleness, damage_out, mises_out,
    kappa, stress, labels, damage, mises, in_sem, out_sem, *, step,
):
    cells_x = labels.shape[0]
    chunks = range(0, cells_x, step)
    pairs = ((kappa_in, kappa), (labels_in, labels), (stress_in, stress))
    loads, stores = [], []
    for i, start in enumerate(chunks):
        planes = pl.ds(start, step)
        loads.append([
            pltpu.make_async_copy(src.at[planes], dst.at[planes], in_sem.at[3 * i + k])
            for k, (src, dst) in enumerate(pairs)
        ])
        for copy in loads[-1]:
            copy.start()

    def plane(x):
        masks = phase_masks(labels[x])

        def chosen(ref):
            return jnp.where(
                masks[0], ref[0], jnp.where(masks[1], ref[1], jnp.where(masks[2], ref[2], ref[3]))
            )

        start, ductile, brittle = chosen(threshold), chosen(ductility), chosen(brittleness)
        now = kappa[x]
        grown = (
            1.0
            - start * (1.0 - ductile) / jnp.maximum(now, start)
            - ductile * jnp.exp(brittle * (start - now))
        )
        grown = jnp.where(now > start, grown, 0.0)
        damage[x] = grown
        mises[x] = (1.0 - grown) * stress[x]

    for i, start in enumerate(chunks):
        for copy in loads[i]:
            copy.wait()
        pl.loop(start, start + step)(plane)
        planes = pl.ds(start, step)
        for k, (src, dst) in enumerate(((damage, damage_out), (mises, mises_out))):
            copy = pltpu.make_async_copy(src.at[planes], dst.at[planes], out_sem.at[2 * i + k])
            copy.start()
            stores.append(copy)
    for copy in stores:
        copy.wait()


def shards(
    displacement, applied_strain, labels, history,
    modulus, poisson, threshold, ductility, brittleness, weight,
):
    cells_x, cells_y, cells_z = labels.shape
    half = cells_z // 2
    f32 = functools.partial(pltpu.VMEM, dtype=jnp.float32)
    bf16 = functools.partial(pltpu.VMEM, dtype=jnp.bfloat16)
    full = (cells_x, cells_y, cells_z)
    tile = (pl.cdiv(cells_x * RADIUS, LANES), cells_y, LANES)
    halo_x = f32((2, 2, RADIUS, cells_y, half))
    halo_y = f32((2, 2, cells_x, RADIUS, half))
    wide = cells_z + LANES
    copies = 43
    smem = functools.partial(pltpu.SMEM, dtype=jnp.float32)
    scratch = [
        smem(applied_strain.shape), smem(modulus.shape), smem(poisson.shape), smem(weight.shape),
        f32((3, cells_x + 1, cells_y + ROWS, wide)),
        f32((9, cells_y, cells_z)),
        f32((3, cells_x, ROWS, cells_z)),
        f32((3, cells_x, cells_z)),
        f32((3, cells_x, wide)),
        f32((3, ROWS, wide)),
        pltpu.VMEM(full, jnp.int32),
        f32(full), f32(full),
        f32((16, cells_z)),
        bf16((cells_z + 2 * LANES, cells_z)), bf16((cells_z + 2 * LANES, cells_z)),
        f32(full), f32(full), f32(full), f32(full), f32(full), f32(full), f32(full), f32(full),
        halo_x, halo_y, halo_x, halo_y, halo_x, halo_y, halo_x, halo_y,
        f32((2,) + tile), f32((2,) + tile),
        f32(tile), f32(tile), f32(tile), f32(tile),
        pltpu.SemaphoreType.DMA((8,)),
        pltpu.SemaphoreType.DMA((1 + cells_x // RADIUS,)),
        pltpu.SemaphoreType.DMA((copies,)),
        pltpu.SemaphoreType.DMA((copies,)),
    ]
    whole = pl.BlockSpec(memory_space=pl.ANY)
    scalars = pl.BlockSpec(memory_space=pltpu.SMEM)
    out = jax.ShapeDtypeStruct(full, jnp.float32)
    kappa, stress = pl.pallas_call(
        kernel,
        out_shape=(out, out),
        in_specs=[whole] * 7,
        out_specs=(whole, whole),
        scratch_shapes=scratch,
        compiler_params=pltpu.CompilerParams(
            collective_id=0, has_side_effects=True, vmem_limit_bytes=56 * 1024 * 1024
        ),
        name="strain_and_average",
    )(displacement, labels, history, applied_strain, modulus, poisson, weight)
    step = 8
    chunks = cells_x // step
    return pl.pallas_call(
        functools.partial(finish, step=step),
        out_shape=(out, out),
        in_specs=[whole] * 3 + [scalars] * 3,
        out_specs=(whole, whole),
        scratch_shapes=[
            f32(full), f32(full), pltpu.VMEM(full, jnp.int32), f32(full), f32(full),
            pltpu.SemaphoreType.DMA((3 * chunks,)),
            pltpu.SemaphoreType.DMA((2 * chunks,)),
        ],
        compiler_params=pltpu.CompilerParams(vmem_limit_bytes=56 * 1024 * 1024),
        name="damage_and_stress",
    )(kappa, stress, labels, threshold, ductility, brittleness)


def solution(mesh):
    block = P("gx", "gy", "gz")
    placed = (P(None, "gx", "gy", "gz"), P(), block, block, P(), P(), P(), P(), P(), P())
    return jax.shard_map(
        shards, mesh=mesh, in_specs=placed, out_specs=(block, block), check_vma=False
    )
```
